128 devices in a mesh: gx: 8 (over z, core), gy: 16 (over x, y).
Axes of the slice: x: 4, y: 4, z: 4, core: 2. Of those that a mesh axis runs over, the one named last changes fastest.
Arguments:
- velocity: float32 [256, 512, 3, 256], P('gx', 'gy'), may hold values from -6 to 6
- fiber_loads: float32 [3, 786432], P(None, ('gx', 'gy')), may hold values from -96 to 96
- fractions: float32 [3, 786432], P(None, ('gx', 'gy')), may hold values from 0 to 1
- corners: int32 [3, 786432], P(None, ('gx', 'gy')), may hold values from 0 to 511, as said below
- neighbours: int32 [786432], P(('gx', 'gy')), may hold values from 0 to 6143
- counts: int32 [16384], P(('gx', 'gy')), may hold values from 1 to 48, as said below
Outputs:
- velocity_next: float32 [256, 512, 3, 256], P('gx', 'gy')
- fiber_velocity: float32 [3, 786432], P(None, ('gx', 'gy'))
The draws below stay inside these ranges and needn't reach their ends.
Inputs may be any that keep to these rules, and one draw needn't show every extreme that they name: `counts`: in every draw some destination device receives 48 live slots from every source device. For a slot whose destination device has x block a and y block b: corners[0] is a * 32 + o mod 256 with o from -2 to 30, corners[1] is b * 32 + o mod 512 with o from -2 to 30, corners[2] any cell along z.
All inputs are finite; a program needn't handle non-finite values.
Results may differ from the reference program's by a relative error of at most 0.0029.
Values may be sent and summed in bfloat16 or wider, within the bound.
A program may use at most 128 MiB of HBM per device.

```python
import jax
import jax.numpy as jnp
from jax import lax

CX = 32
CY = 32
NZ = 256
CAP = 48
NX = 256
NY = 512
SLOTS = 786432
N_GX = 8
N_GY = 16


def draw_counts(key, part):
    devices = N_GX * N_GY
    first, second = jax.random.split(jax.random.fold_in(key, 11))
    table = jax.random.randint(first, (devices, devices), 1, CAP + 1)
    chosen = jax.random.randint(second, (), 0, devices)
    table = jnp.where(jnp.arange(devices)[None, :] == chosen, CAP, table)
    return table.reshape(-1).astype(jnp.int32)


def draw_corners(key, part):
    devices = N_GX * N_GY
    total = devices * devices * CAP
    first, second, third = jax.random.split(jax.random.fold_in(key, 23), 3)
    slot_ids = jnp.arange(total, dtype=jnp.int32)
    target = slot_ids // CAP % devices
    block_x = target // N_GY
    block_y = target % N_GY
    corner_x = (block_x * CX + jax.random.randint(first, (total,), -2, CX - 1)) % NX
    corner_y = (block_y * CY + jax.random.randint(second, (total,), -2, CY - 1)) % NY
    corner_z = jax.random.randint(third, (total,), 0, NZ)
    return jnp.stack([corner_x, corner_y, corner_z]).astype(jnp.int32)


def set_ends(values, rng, smallest, high):
    longest = values.shape.index(max(values.shape))
    spots = []
    for shift in (0, 1):
        where = [jax.random.randint(jax.random.fold_in(rng, axis), (), 0, length) for axis, length in enumerate(values.shape)]
        where[longest] = (where[longest] + shift) % values.shape[longest]
        spots.append(tuple(where))
    return values.at[spots[0]].set(smallest).at[spots[1]].set(high)


def shard_levels(stream_key, shape, cuts, least, largest):
    loudness = 1.0
    for dim, shards_of in cuts:
        heights = jax.random.uniform(jax.random.fold_in(jax.random.fold_in(stream_key, 6), dim), (shards_of,), jnp.float32, least / len(cuts), largest / len(cuts))
        loudness = loudness * jnp.repeat(jnp.exp(heights), shape[dim] // shards_of).reshape((-1,) + (1,) * (len(shape) - 1 - dim))
    return loudness


def bell_draw(own_key, shape, deviation, limit, cuts=(), held_as=jnp.bfloat16):
    entries = jax.random.normal(own_key, shape, jnp.float32) * deviation
    if len(cuts) > 0:
        entries = shard_levels(own_key, shape, cuts, -0.22, 0.18) * entries
    return jnp.clip(entries, min=-limit, max=limit).astype(held_as)


def setup_inputs(seed: int = 0) -> dict:
    key_list = jax.random.split(jax.random.key(seed), 7)
    velocity = bell_draw(key_list[0], (NX, NY, 3, NZ), 1.0, 6.0, ((0, 8), (1, 16)), jnp.float32)
    fiber_loads = bell_draw(key_list[1], (3, SLOTS), 16.0, 96.0, ((1, 128),), jnp.float32)
    fractions = jnp.clip(1.0 * jax.random.uniform(key_list[2], (3, SLOTS), jnp.float32) ** shard_levels(key_list[2], (3, SLOTS), ((1, 128),), -0.2, 0.2), 0.0, 1.0)
    corners = draw_corners(jax.random.fold_in(key_list[6], 71), 0)
    neighbours = set_ends(jax.random.randint(key_list[4], (SLOTS,), 0, CAP * N_GX * N_GY), jax.random.fold_in(key_list[4], 1), 0, (CAP * N_GX * N_GY) - 1).astype(jnp.int32)
    counts = draw_counts(jax.random.fold_in(key_list[6], 71), 0)
    return dict(velocity=velocity, fiber_loads=fiber_loads, fractions=fractions, corners=corners, neighbours=neighbours, counts=counts)


viscosity = 0.15


def peskin(fraction):
    nodes = jnp.arange(4, dtype=jnp.float32).reshape((4,) + (1,) * fraction.ndim)
    return 0.25 * (1.0 + jnp.cos(0.5 * jnp.pi * (1.0 + fraction[None] - nodes)))


def laplace_of(field):
    result = jnp.roll(field, -1, 0) + jnp.roll(field, 1, 0)
    result = result + jnp.roll(field, -1, 1) + jnp.roll(field, 1, 1)
    result = result + jnp.roll(field, -1, 3) + jnp.roll(field, 1, 3)
    return result - 6.0 * field


def to_bf16(values):
    return lax.optimization_barrier(values.astype(jnp.bfloat16)).astype(jnp.float32)


def reference(velocity, fiber_loads, fractions, corners, neighbours, counts):
    devices = N_GX * N_GY
    total = devices * devices * CAP
    slot_ids = jnp.arange(total, dtype=jnp.int32)
    live_mask = (jnp.arange(CAP, dtype=jnp.int32)[None, :] < counts[:, None]).reshape(-1).astype(jnp.float32)
    position = corners.astype(jnp.float32) + fractions
    owner_base = (slot_ids // (devices * CAP)) * (devices * CAP)
    partner = (owner_base + neighbours).astype(jnp.int32)
    stiffness = jnp.array([2.0 / NX, 2.0 / NY, 2.0 / NZ], jnp.float32)[:, None]
    forcing = (fiber_loads + stiffness * (position[:, partner] - position)) * live_mask
    weight_x = peskin(fractions[0])
    weight_y = peskin(fractions[1])
    weight_z = peskin(fractions[2])
    component = jnp.arange(3, dtype=jnp.int32)

    def place(offset):
        step_i = offset // 16
        step_j = (offset // 4) % 4
        step_k = offset % 4
        cell_x = (corners[0] + step_i) % NX
        cell_y = (corners[1] + step_j) % NY
        cell_z = (corners[2] + step_k) % NZ
        plane_wts = to_bf16(weight_x[step_i] * weight_y[step_j])
        return cell_x, cell_y, cell_z, plane_wts, weight_z[step_k]

    def spread_step(grid_sum, offset):
        cell_x, cell_y, cell_z, plane_wts, depth_wts = place(offset)
        push_rows = to_bf16(forcing * depth_wts[None, :])
        values = plane_wts[None, :] * push_rows
        grid_sum = grid_sum.at[cell_x[None, :], cell_y[None, :], component[:, None], cell_z[None, :]].add(values)
        return grid_sum, None

    grid_sum, _ = lax.scan(spread_step, jnp.zeros((NX, NY, 3, NZ), jnp.float32), jnp.arange(64, dtype=jnp.int32))
    field = velocity + grid_sum
    for sweep in range(2):
        field = field + viscosity * laplace_of(field)
    rounded = to_bf16(field)

    def gather_step(running, offset):
        cell_x, cell_y, cell_z, plane_wts, depth_wts = place(offset)
        picked = rounded[cell_x[:, None], cell_y[:, None], component[None, :], cell_z[:, None]].T
        return running + plane_wts[None, :] * picked * depth_wts[None, :], None

    running, _ = lax.scan(gather_step, jnp.zeros((3, total), jnp.float32), jnp.arange(64, dtype=jnp.int32))
    return field, running * live_mask
```

```python
import functools

import jax
import jax.numpy as jnp
from jax import lax
from jax.experimental import pallas as pl
from jax.experimental.pallas import tpu as pltpu
from jax.sharding import PartitionSpec as P

viscosity = 0.15
GX, GY = 8, 16
DEVICES = GX * GY
CAP = 48
SLOTS = CAP * DEVICES
CELLS = 32
NZ = 256
EXT = 40
ROWS = 36 * EXT
BLOCKS = CAP // 2
MESH = pl.DeviceIdType.MESH
VMEM = pl.BlockSpec(memory_space=pltpu.VMEM)
ANY = pl.BlockSpec(memory_space=pl.ANY)
f32, bf16, i32 = jnp.float32, jnp.bfloat16, jnp.int32


def params(mib=16, **more):
    return pltpu.CompilerParams(vmem_limit_bytes=mib * 2**20, **more)


def prep_kernel(loads_ref, frac_ref, corner_ref, partner_ref, counts_ref, out_ref, flat_ref, pos_ref):
    def flat_rows(ref, c):
        for r in range(CAP):
            flat_ref[r : r + 1, :] = ref[c : c + 1, 128 * r : 128 * r + 128].astype(f32)
        return flat_ref[...]

    lane = lax.broadcasted_iota(i32, (CAP, 128), 1)
    flat_id = lax.broadcasted_iota(i32, (CAP, 128), 0) * 128 + lane
    bucket = (flat_id * 43691) >> 21
    partner = partner_ref[...]
    high, low = partner >> 7, partner & 127
    whole = (CELLS * GX, CELLS * GY, NZ)
    for c in range(3):
        fraction = flat_rows(frac_ref, c)
        corner = flat_rows(corner_ref, c)
        loads = flat_rows(loads_ref, c)
        position = corner + fraction
        flat_ref[...] = position
        gathered = jnp.zeros((CAP, 128), f32)
        for r in range(CAP):
            row = jnp.broadcast_to(flat_ref[r : r + 1, :], (CAP, 128))
            taken = jnp.take_along_axis(row, low, axis=1, mode="promise_in_bounds")
            gathered = jnp.where(high == r, taken, gathered)
        forcing = loads + (2.0 / whole[c]) * (gathered - position)
        pos_ref[c * CAP : c * CAP + CAP, :] = forcing
        cell = corner.astype(i32)
        if c == 0:
            cell = (cell - (bucket >> 4) * CELLS + 4) & (whole[0] - 1)
        if c == 1:
            cell = (cell - (bucket & 15) * CELLS + 4) & (whole[1] - 1)
        pos_ref[(3 + c) * CAP : (3 + c) * CAP + CAP, :] = cell.astype(f32) + fraction

    lane = lax.broadcasted_iota(i32, (16, 128), 1)
    for j in range(8):
        row0, lane0 = divmod(CAP * j, 128)
        live = (lane & 63) < counts_ref[pl.ds(j, 16, stride=8), :]

        def piece(v, target):
            part = pos_ref[pl.ds(v * CAP + row0, 16, stride=3), :]
            if lane0 + CAP > 128:
                later = pos_ref[pl.ds(v * CAP + row0 + 1, 16, stride=3), :]
                part = jnp.where(lane >= lane0, part, later)
            shift = (target - lane0) % 128
            return pltpu.roll(part, shift, 1) if shift else part

        for pair in range(3):
            row = jnp.where(lane < 64, piece(2 * pair, 0), piece(2 * pair + 1, 64))
            if pair == 0:
                row = jnp.where(live, row, 0.0)
            if pair == 1:
                row = jnp.where(live | (lane >= 64), row, 0.0)
            out_ref[pl.ds(4 * j + pair, 16, stride=32), :] = row
        out_ref[pl.ds(4 * j + 3, 16, stride=32), :] = jnp.zeros((16, 128), f32)


def greet(peers):
    barrier = pltpu.get_barrier_semaphore()
    for peer in peers:
        pl.semaphore_signal(barrier, inc=1, device_id=peer, device_id_type=MESH)
    pl.semaphore_wait(barrier, len(peers))


def two_stage(first_axis, first, second_axis, second, x_ref, out_ref, mid_ref, send1, recv1, send2, recv2, here):
    me1, me2 = lax.axis_index(first_axis), lax.axis_index(second_axis)
    greet(
        [{first_axis: lax.rem(me1 + k, first)} for k in range(1, first)]
        + [{second_axis: lax.rem(me2 + k, second)} for k in range(1, second)]
    )
    copies = []
    for k in range(1, first):
        peer = lax.rem(me1 + k, first)
        copy = pltpu.make_async_remote_copy(
            src_ref=x_ref.at[peer],
            dst_ref=mid_ref.at[me1],
            send_sem=send1.at[k],
            recv_sem=recv1.at[k],
            device_id={first_axis: peer},
            device_id_type=MESH,
        )
        copy.start()
        copies.append(copy)
    own = pltpu.make_async_copy(x_ref.at[me1], mid_ref.at[me1], here.at[0])
    own.start()
    own.wait()
    for copy in copies:
        copy.wait_recv()
    for k in range(1, second):
        peer = lax.rem(me2 + k, second)
        copy = pltpu.make_async_remote_copy(
            src_ref=mid_ref.at[:, peer],
            dst_ref=out_ref.at[me2],
            send_sem=send2.at[k],
            recv_sem=recv2.at[k],
            device_id={second_axis: peer},
            device_id_type=MESH,
        )
        copy.start()
        copies.append(copy)
    own = pltpu.make_async_copy(mid_ref.at[:, me2], out_ref.at[me2], here.at[1])
    own.start()
    own.wait()
    for copy in copies[first - 1 :]:
        copy.wait_recv()
    for copy in copies:
        copy.wait_send()


def exchange(x, first_axis, first, second_axis, second, rows, identity):
    kernel = functools.partial(two_stage, first_axis, first, second_axis, second)
    return pl.pallas_call(
        kernel,
        out_shape=jax.ShapeDtypeStruct((second, first, rows, 128), f32),
        in_specs=[VMEM],
        out_specs=VMEM,
        scratch_shapes=[
            pltpu.VMEM((first, second, rows, 128), f32),
            pltpu.SemaphoreType.DMA((first,)),
            pltpu.SemaphoreType.DMA((first,)),
            pltpu.SemaphoreType.DMA((second,)),
            pltpu.SemaphoreType.DMA((second,)),
            pltpu.SemaphoreType.DMA((2,)),
        ],
        compiler_params=params(collective_id=identity, has_side_effects=True),
    )(x.reshape(first, second, rows, 128))


SIDES = ((-1, 0), (1, 0), (0, -1), (0, 1), (-1, -1), (-1, 1), (1, -1), (1, 1))
LOW, HIGH = (2, 8), (32, 38)


def side_rows(side):
    dx, dy = side
    return 6 * EXT if dy == 0 else 36 * 8 if dx == 0 else 6 * 8


def halo_kernel(*refs):
    sent, got, (send, recv) = refs[:8], refs[8:16], refs[16:]
    x, y = lax.axis_index("gx"), lax.axis_index("gy")
    peers = [(lax.rem(x + dx + GX, GX), lax.rem(y + dy + GY, GY)) for dx, dy in SIDES]
    greet(peers)
    copies = []
    for k in range(8):
        copy = pltpu.make_async_remote_copy(
            src_ref=sent[k],
            dst_ref=got[k],
            send_sem=send.at[k],
            recv_sem=recv.at[k],
            device_id=peers[k],
            device_id_type=MESH,
        )
        copy.start()
        copies.append(copy)
    for copy in copies:
        copy.wait_recv()
    for copy in copies:
        copy.wait_send()


def halo_exchange(strips):
    return pl.pallas_call(
        halo_kernel,
        out_shape=[jax.ShapeDtypeStruct(s.shape, s.dtype) for s in strips],
        in_specs=[VMEM] * 8,
        out_specs=[VMEM] * 8,
        scratch_shapes=[pltpu.SemaphoreType.DMA((8,)), pltpu.SemaphoreType.DMA((8,))],
        compiler_params=params(collective_id=1, has_side_effects=True),
    )(*strips)


def point_row(ref, base, block):
    return jnp.concatenate([ref[pl.ds(base + 2 * block, 1), :], ref[pl.ds(base + 2 * block + 1, 1), :]], axis=1)


def table(wts_ref, cell_ref, dim, block, length):
    corner = point_row(cell_ref, dim * CAP, block)
    delta = lax.broadcasted_iota(i32, (length, 256), 0) - corner
    if dim == 2:
        delta = delta & (NZ - 1)
    result = jnp.zeros((length, 256), f32)
    for k in range(4):
        result = jnp.where(delta == k, point_row(wts_ref, (4 * dim + k) * CAP, block), result)
    return result


def plane_rows(wts_ref, cell_ref, block, store):
    along_x = table(wts_ref, cell_ref, 0, block, EXT)
    along_y = table(wts_ref, cell_ref, 1, block, EXT)
    for i in range(18):
        x = 2 + 2 * i
        both = jnp.concatenate([along_y * along_x[x : x + 1], along_y * along_x[x + 1 : x + 2]], axis=0)
        store(80 * i, both.astype(bf16))


def spread_kernel(recv_ref, velocity_ref, field_ref, wts_ref, cell_ref, *refs):
    strips, (values_ref, plane_ref, push_ref) = refs[:8], refs[8:]
    for pair in range(3):
        values_ref[128 * pair : 128 * pair + 128, :] = recv_ref[pl.ds(pair, 128, stride=4), :].T
    for dim in range(3):
        position = values_ref[64 * (3 + dim) : 64 * (3 + dim) + CAP, :]
        corner = jnp.floor(position)
        angle = (0.5 * jnp.pi) * (position - corner)
        sine, cosine = jnp.sin(angle), jnp.cos(angle)
        cell_ref[dim * CAP : dim * CAP + CAP, :] = corner.astype(i32)
        for k, term in enumerate((-sine, cosine, sine, -cosine)):
            at = (4 * dim + k) * CAP
            wts_ref[at : at + CAP, :] = 0.25 * (1.0 + term)

    def fill(block, _):
        columns = pl.ds(pl.multiple_of(block * 256, 256), 256)

        def store(row, both):
            plane_ref[row : row + 80, columns] = both

        plane_rows(wts_ref, cell_ref, block, store)
        depth = table(wts_ref, cell_ref, 2, block, NZ)
        for c in range(3):
            push_ref[c, :, columns] = (depth * point_row(values_ref, 64 * c, block)).astype(bf16)
        return 0

    lax.fori_loop(0, BLOCKS, fill, 0)

    def component(c, _):
        base = c * EXT
        empty = jnp.zeros((2, EXT, NZ), f32)
        field_ref[pl.ds(base, 2)] = empty
        field_ref[pl.ds(base + 38, 2)] = empty
        push = push_ref[c]

        for half in range(2):
            part = lax.dot_general(
                plane_ref[720 * half : 720 * half + 720, :], push, (((1,), (1,)), ((), ())), preferred_element_type=f32
            )
            field_ref[pl.ds(base + 2 + 18 * half, 18)] = part.reshape(18, EXT, NZ)

        def own(x, _):
            field_ref[base + 4 + x, 4:36, :] += velocity_ref[c * CELLS + x]
            return 0

        lax.fori_loop(0, CELLS, own, 0)
        for side, strip in zip(SIDES, strips):
            dx, dy = side
            first, last = (2, 38) if dx == 0 else LOW if dx < 0 else HIGH
            low, high = (0, EXT) if dy == 0 else (0, 8) if dy < 0 else (32, 40)
            part = field_ref[pl.ds(base + first, last - first), low:high, :]
            strip[c] = part.reshape(side_rows(side), NZ).astype(bf16)
        return 0

    lax.fori_loop(0, 3, component, 0)


def spread(received, velocity):
    shapes = [
        jax.ShapeDtypeStruct((3 * EXT, EXT, NZ), f32),
        jax.ShapeDtypeStruct((12 * CAP, 128), f32),
        jax.ShapeDtypeStruct((3 * CAP, 128), i32),
    ] + [jax.ShapeDtypeStruct((3, side_rows(side), NZ), bf16) for side in SIDES]
    return pl.pallas_call(
        spread_kernel,
        out_shape=shapes,
        in_specs=[VMEM, VMEM],
        out_specs=[VMEM] * len(shapes),
        scratch_shapes=[
            pltpu.VMEM((384, 128), f32),
            pltpu.VMEM((ROWS, SLOTS), bf16),
            pltpu.VMEM((3, NZ, SLOTS), bf16),
        ],
        compiler_params=params(56),
        cost_estimate=pl.CostEstimate(flops=2 * ROWS * SLOTS * 3 * NZ, bytes_accessed=10**7, transcendentals=0),
    )(received, velocity)


def laplace(ref, x):
    center = ref[x]
    result = ref[x - 1] + ref[x + 1]
    result = result + pltpu.roll(center, 1, 0) + pltpu.roll(center, EXT - 1, 0)
    result = result + pltpu.roll(center, 1, 1) + pltpu.roll(center, NZ - 1, 1)
    return center + viscosity * (result - 6.0 * center)


def sample_kernel(field_ref, wts_ref, cell_ref, *refs):
    got, (next_ref, out_ref, v0_ref, v1_ref, v2_ref, across_ref, plane_ref, sum_ref) = refs[:8], refs[8:]
    v2_ref[ROWS:, :] = jnp.zeros((1536 - ROWS, NZ), f32)
    plane_ref[ROWS:, :] = jnp.zeros((1536 - ROWS, 256), bf16)

    def component(c, _):
        v0_ref[...] = field_ref[pl.ds(c * EXT, EXT)]
        for side, strip in zip(SIDES, got):
            dx, dy = side
            count = 36 if dx == 0 else 6
            first = 2 if dx == 0 else 34 if dx < 0 else 0
            low, high = (0, EXT) if dy == 0 else (32, 40) if dy < 0 else (0, 8)
            v0_ref[first : first + count, low:high, :] += strip[c].astype(f32).reshape(count, high - low, NZ)

        def first_sweep(x, _):
            v1_ref[x] = laplace(v0_ref, x)
            return 0

        lax.fori_loop(1, EXT - 1, first_sweep, 0)

        def second_sweep(x, _):
            value = laplace(v1_ref, x)
            v2_ref[pl.ds(pl.multiple_of((x - 2) * EXT, 8), EXT), :] = value

            @pl.when((x >= 4) & (x < 36))
            def _():
                next_ref[c * CELLS + x - 4] = value[4:36]

            return 0

        lax.fori_loop(2, EXT - 2, second_sweep, 0)
        for part in range(12):
            piece = v2_ref[128 * part : 128 * part + 128, :]
            across_ref[c, :, 128 * part : 128 * part + 128] = piece.T.astype(bf16)
        return 0

    v1_ref[0] = jnp.zeros((EXT, NZ), f32)
    v1_ref[EXT - 1] = jnp.zeros((EXT, NZ), f32)
    lax.fori_loop(0, 3, component, 0)

    def interpolate(block, _):
        def store(row, both):
            plane_ref[row : row + 80, :] = both

        plane_rows(wts_ref, cell_ref, block, store)
        depth = table(wts_ref, cell_ref, 2, block, NZ)
        for c in range(3):
            mixed = jnp.dot(across_ref[c], plane_ref[...], preferred_element_type=f32)
            total = jnp.sum(mixed * depth, axis=0, keepdims=True)
            sum_ref[pl.ds(64 * c + 2 * block, 1), :] = total[:, :128]
            sum_ref[pl.ds(64 * c + 2 * block + 1, 1), :] = total[:, 128:]
        return 0

    sum_ref[...] = jnp.zeros((256, 128), f32)
    lax.fori_loop(0, BLOCKS, interpolate, 0)
    out_ref[pl.ds(0, 128, stride=2), :] = sum_ref[0:128, :].T
    out_ref[pl.ds(1, 128, stride=2), :] = sum_ref[128:256, :].T


def sample(field, wts, cells, got):
    return pl.pallas_call(
        sample_kernel,
        out_shape=[
            jax.ShapeDtypeStruct((3 * CELLS, CELLS, NZ), f32),
            jax.ShapeDtypeStruct((256, 128), f32),
        ],
        in_specs=[VMEM] * 11,
        out_specs=[VMEM] * 2,
        scratch_shapes=[
            pltpu.VMEM((EXT, EXT, NZ), f32),
            pltpu.VMEM((EXT, EXT, NZ), f32),
            pltpu.VMEM((1536, NZ), f32),
            pltpu.VMEM((3, NZ, 1536), bf16),
            pltpu.VMEM((1536, 256), bf16),
            pltpu.VMEM((256, 128), f32),
        ],
        compiler_params=params(48),
        cost_estimate=pl.CostEstimate(flops=2 * 1536 * SLOTS * 3 * NZ, bytes_accessed=10**7, transcendentals=0),
    )(field, wts, cells, *got)


def unpack_kernel(back_ref, counts_ref, out_ref, flat_ref):
    lane = lax.broadcasted_iota(i32, (16, 128), 1)
    for c in range(3):
        base = 64 * (c % 2)
        rows = [jnp.zeros((16, 128), f32)] * 3
        for j in range(8):
            row0, lane0 = divmod(CAP * j, 128)
            part = back_ref[pl.ds(2 * j + c // 2, 16, stride=16), :]
            part = jnp.where(lane - base < counts_ref[pl.ds(j, 16, stride=8), :], part, 0.0)
            shift = (lane0 - base) % 128
            part = pltpu.roll(part, shift, 1) if shift else part
            rows[row0] = jnp.where((lane >= lane0) & (lane < lane0 + CAP), part, rows[row0])
            if lane0 + CAP > 128:
                rows[row0 + 1] = jnp.where(lane < lane0 + CAP - 128, part, rows[row0 + 1])
        for r in range(3):
            flat_ref[pl.ds(c * CAP + r, 16, stride=3), :] = rows[r]
        for r in range(CAP):
            out_ref[c : c + 1, 128 * r : 128 * r + 128] = flat_ref[c * CAP + r : c * CAP + r + 1, :]


def body(velocity, fiber_loads, fractions, corners, neighbours, counts):
    counts = counts.reshape(DEVICES, 1)
    payload = pl.pallas_call(
        prep_kernel,
        out_shape=jax.ShapeDtypeStruct((4 * DEVICES, 128), f32),
        in_specs=[VMEM] * 5,
        out_specs=VMEM,
        scratch_shapes=[pltpu.VMEM((CAP, 128), f32), pltpu.VMEM((6 * CAP, 128), f32)],
        compiler_params=params(),
    )(fiber_loads, fractions, corners, neighbours.reshape(CAP, 128), counts)
    received = exchange(payload, "gx", GX, "gy", GY, 4, 0).reshape(4 * DEVICES, 128)
    mine = velocity.transpose(2, 0, 1, 3).reshape(3 * CELLS, CELLS, NZ)
    field, wts, cells, *strips = spread(received, mine)
    got = halo_exchange(strips)
    following, samples = sample(field, wts, cells, got)
    back = exchange(samples, "gy", GY, "gx", GX, 2, 2).reshape(2 * DEVICES, 128)
    fiber_velocity = pl.pallas_call(
        unpack_kernel,
        out_shape=jax.ShapeDtypeStruct((3, SLOTS), f32),
        in_specs=[VMEM] * 2,
        out_specs=VMEM,
        scratch_shapes=[pltpu.VMEM((3 * CAP, 128), f32)],
        compiler_params=params(),
    )(back, counts)
    velocity_next = following.reshape(3, CELLS, CELLS, NZ).transpose(1, 2, 0, 3)
    return (velocity_next, fiber_velocity)


def solution(mesh):
    return jax.shard_map(
        body,
        mesh=mesh,
        in_specs=(
            P("gx", "gy", None, None),
            P(None, ("gx", "gy")),
            P(None, ("gx", "gy")),
            P(None, ("gx", "gy")),
            P(("gx", "gy")),
            P(("gx", "gy")),
        ),
        out_specs=(P("gx", "gy", None, None), P(None, ("gx", "gy"))),
        check_vma=False,
    )
```

```python
import functools

import jax
import jax.numpy as jnp
from jax import lax
from jax.experimental import pallas as pl
from jax.experimental.pallas import tpu as pltpu
from jax.sharding import PartitionSpec as P

viscosity = 0.15
GX, GY = 8, 16
DEVICES = GX * GY
CAP = 48
SLOTS = CAP * DEVICES
CELLS = 32
NZ = 256
EXT = 40
ROWS = 36 * EXT
PADDED = 1536
BLOCKS = CAP // 2
MESH = pl.DeviceIdType.MESH
VMEM = pl.BlockSpec(memory_space=pltpu.VMEM)
ANY = pl.BlockSpec(memory_space=pl.ANY)
f32, bf16, i32 = jnp.float32, jnp.bfloat16, jnp.int32


def params(mib=16, **more):
    return pltpu.CompilerParams(vmem_limit_bytes=mib * 2**20, **more)


def fetch(pairs, sems):
    copies = [pltpu.make_async_copy(src, dst, sems.at[k]) for k, (src, dst) in enumerate(pairs)]
    for copy in copies:
        copy.start()
    for copy in copies:
        copy.wait()


def counts_column(counts_ref):
    return jnp.broadcast_to(counts_ref[...].astype(f32), (DEVICES, DEVICES)).T.astype(i32)


def prep_kernel(loads_hbm, frac_hbm, corner_hbm, partner_hbm, counts_hbm, out_ref, *scratch):
    loads_ref, frac_ref, corner_ref, partner_ref, counts_ref, sems, live_ref, flat_ref, pos_ref = scratch
    fetch(
        [
            (loads_hbm, loads_ref),
            (frac_hbm, frac_ref),
            (corner_hbm, corner_ref),
            (partner_hbm, partner_ref),
            (counts_hbm, counts_ref),
        ],
        sems,
    )
    live_ref[...] = counts_column(counts_ref)

    def flat_rows(ref, c):
        for r in range(CAP):
            flat_ref[r : r + 1, :] = ref[c : c + 1, 128 * r : 128 * r + 128].astype(f32)
        return flat_ref[...]

    lane = lax.broadcasted_iota(i32, (CAP, 128), 1)
    flat_id = lax.broadcasted_iota(i32, (CAP, 128), 0) * 128 + lane
    bucket = (flat_id * 43691) >> 21
    partner = partner_ref[...]
    high, low = partner >> 7, partner & 127
    whole = (CELLS * GX, CELLS * GY, NZ)
    for c in range(3):
        fraction = flat_rows(frac_ref, c)
        corner = flat_rows(corner_ref, c)
        loads = flat_rows(loads_ref, c)
        position = corner + fraction
        flat_ref[...] = position
        gathered = jnp.zeros((CAP, 128), f32)
        for r in range(CAP):
            row = jnp.broadcast_to(flat_ref[r : r + 1, :], (CAP, 128))
            taken = jnp.take_along_axis(row, low, axis=1, mode="promise_in_bounds")
            gathered = jnp.where(high == r, taken, gathered)
        forcing = loads + (2.0 / whole[c]) * (gathered - position)
        pos_ref[c * CAP : c * CAP + CAP, :] = forcing
        cell = corner.astype(i32)
        if c == 0:
            cell = (cell - (bucket >> 4) * CELLS + 4) & (whole[0] - 1)
        if c == 1:
            cell = (cell - (bucket & 15) * CELLS + 4) & (whole[1] - 1)
        pos_ref[(3 + c) * CAP : (3 + c) * CAP + CAP, :] = cell.astype(f32) + fraction

    lane = lax.broadcasted_iota(i32, (16, 128), 1)
    for j in range(8):
        row0, lane0 = divmod(CAP * j, 128)
        live = (lane & 63) < live_ref[pl.ds(j, 16, stride=8), :]

        def piece(v, target):
            part = pos_ref[pl.ds(v * CAP + row0, 16, stride=3), :]
            if lane0 + CAP > 128:
                later = pos_ref[pl.ds(v * CAP + row0 + 1, 16, stride=3), :]
                part = jnp.where(lane >= lane0, part, later)
            shift = (target - lane0) % 128
            return pltpu.roll(part, shift, 1) if shift else part

        for pair in range(3):
            row = jnp.where(lane < 64, piece(2 * pair, 0), piece(2 * pair + 1, 64))
            if pair == 0:
                row = jnp.where(live, row, 0.0)
            if pair == 1:
                row = jnp.where(live | (lane >= 64), row, 0.0)
            out_ref[pl.ds(4 * j + pair, 16, stride=32), :] = row
        out_ref[pl.ds(4 * j + 3, 16, stride=32), :] = jnp.zeros((16, 128), f32)


def send(src, dst, sems, at, peer):
    copy = pltpu.make_async_remote_copy(
        src_ref=src,
        dst_ref=dst,
        send_sem=sems[0].at[at],
        recv_sem=sems[1].at[at],
        device_id=peer,
        device_id_type=MESH,
    )
    copy.start()
    return copy


def two_stage(first_axis, first, second_axis, second, x_ref, mid_ref, out_ref, sems1, sems2, here):
    me1, me2 = lax.axis_index(first_axis), lax.axis_index(second_axis)
    own = pltpu.make_async_copy(x_ref.at[me1], mid_ref.at[me1], here.at[0])
    copies = []
    for k in range(1, first):
        peer = lax.rem(me1 + k, first)
        copies.append(send(x_ref.at[peer], mid_ref.at[me1], sems1, k, {first_axis: peer}))
    own.start()
    own.wait()
    for copy in copies:
        copy.wait_recv()
    own = pltpu.make_async_copy(mid_ref.at[:, me2], out_ref.at[me2], here.at[1])
    later = []
    for k in range(1, second):
        peer = lax.rem(me2 + k, second)
        later.append(send(mid_ref.at[:, peer], out_ref.at[me2], sems2, k, {second_axis: peer}))
    own.start()
    own.wait()
    for copy in later:
        copy.wait_recv()
    for copy in copies + later:
        copy.wait_send()


SIDES = ((-1, 0), (1, 0), (0, -1), (0, 1), (-1, -1), (-1, 1), (1, -1), (1, 1))
LOW, HIGH = (2, 8), (32, 38)


def side_rows(side):
    dx, dy = side
    return 6 * EXT if dy == 0 else 36 * 8 if dx == 0 else 6 * 8


def point_row(ref, base, block):
    return jnp.concatenate([ref[pl.ds(base + 2 * block, 1), :], ref[pl.ds(base + 2 * block + 1, 1), :]], axis=1)


def table(wts_ref, cell_ref, dim, block, length):
    corner = point_row(cell_ref, dim * CAP, block)
    delta = lax.broadcasted_iota(i32, (length, 256), 0) - corner
    if dim == 2:
        delta = delta & (NZ - 1)
    result = jnp.zeros((length, 256), f32)
    for k in range(4):
        result = jnp.where(delta == k, point_row(wts_ref, (4 * dim + k) * CAP, block), result)
    return result


def weights(values_ref, wts_ref, cell_ref):
    for dim in range(3):
        position = values_ref[64 * (3 + dim) : 64 * (3 + dim) + CAP, :]
        corner = jnp.floor(position)
        angle = (0.5 * jnp.pi) * (position - corner)
        sine, cosine = jnp.sin(angle), jnp.cos(angle)
        cell_ref[dim * CAP : dim * CAP + CAP, :] = corner.astype(i32)
        for k, term in enumerate((-sine, cosine, sine, -cosine)):
            at = (4 * dim + k) * CAP
            wts_ref[at : at + CAP, :] = 0.25 * (1.0 + term)


def fill_tables(values_ref, wts_ref, cell_ref, plane_ref, push_ref, depth_ref):
    def fill(block, _):
        columns = pl.ds(pl.multiple_of(block * 256, 256), 256)
        along_x = table(wts_ref, cell_ref, 0, block, EXT)
        along_y = table(wts_ref, cell_ref, 1, block, EXT)
        for i in range(18):
            x = 2 + 2 * i
            both = jnp.concatenate([along_y * along_x[x : x + 1], along_y * along_x[x + 1 : x + 2]], axis=0)
            plane_ref[80 * i : 80 * i + 80, columns] = both.astype(bf16)
        depth = table(wts_ref, cell_ref, 2, block, NZ)
        depth_ref[:, columns] = depth
        for c in range(3):
            push_ref[c, :, columns] = (depth * point_row(values_ref, 64 * c, block)).astype(bf16)
        return 0

    plane_ref[ROWS:, :] = jnp.zeros((PADDED - ROWS, SLOTS), bf16)
    lax.fori_loop(0, BLOCKS, fill, 0)


def laplace(ref, x):
    center = ref[x]
    around = ref[x - 1] + ref[x + 1]
    around = around + pltpu.roll(center, 1, 0) + pltpu.roll(center, EXT - 1, 0)
    around = around + pltpu.roll(center, 1, 1) + pltpu.roll(center, NZ - 1, 1)
    return (1.0 - 6.0 * viscosity) * center + viscosity * around


def spread(c, velocity_ref, plane_ref, push_ref, field_ref, strips):
    field = field_ref.at[c]
    empty = jnp.zeros((2, EXT, NZ), f32)
    field[0:2] = empty
    field[38:40] = empty
    for half in range(2):
        part = lax.dot_general(
            plane_ref[720 * half : 720 * half + 720, :],
            push_ref[c],
            (((1,), (1,)), ((), ())),
            preferred_element_type=f32,
        )
        field[2 + 18 * half : 20 + 18 * half] = part.reshape(18, EXT, NZ)

    def own(t, _):
        for k in range(8):
            x = t * 8 + k
            field[4 + x, 4:36, :] += velocity_ref[c * CELLS + x]
        return 0

    lax.fori_loop(0, CELLS // 8, own, 0)
    for side, strip in zip(SIDES, strips):
        dx, dy = side
        first, last = (2, 38) if dx == 0 else LOW if dx < 0 else HIGH
        low, high = (0, EXT) if dy == 0 else (0, 8) if dy < 0 else (32, 40)
        strip[c] = field[first:last, low:high, :].reshape(side_rows(side), NZ).astype(bf16)


def sweep(c, field_ref, got, v1_ref, v2_ref, next_ref, across_ref):
    field = field_ref.at[c]
    for side, strip in zip(SIDES, got):
        dx, dy = side
        count = 36 if dx == 0 else 6
        first = 2 if dx == 0 else 34 if dx < 0 else 0
        low, high = (0, EXT) if dy == 0 else (32, 40) if dy < 0 else (0, 8)
        field[first : first + count, low:high, :] += strip[c].astype(f32).reshape(count, high - low, NZ)

    def first_sweep(t, _):
        for k in range(12):
            x = 1 + t * 12 + k
            v1_ref[x] = laplace(field, x)
        return 0

    lax.fori_loop(0, 3, first_sweep, 0)
    for x in (37, 38):
        v1_ref[x] = laplace(field, x)

    def second(x):
        value = laplace(v1_ref, x)
        v2_ref[pl.ds(pl.multiple_of((x - 2) * EXT, 8), EXT), :] = value
        return value

    for x in (2, 3, 36, 37):
        second(x)

    def second_sweep(t, _):
        for k in range(8):
            x = 4 + t * 8 + k
            next_ref[c * CELLS + x - 4] = second(x)[4:36]
        return 0

    lax.fori_loop(0, 4, second_sweep, 0)
    for part in range(PADDED // 128):
        piece = v2_ref[128 * part : 128 * part + 128, :]
        across_ref[c, :, 128 * part : 128 * part + 128] = piece.T.astype(bf16)


def interpolate(c, across_ref, plane_ref, depth_ref, sum_ref):
    def some(t, _):
        columns = pl.ds(pl.multiple_of(t * 1024, 1024), 1024)
        mixed = jnp.dot(across_ref[c], plane_ref[:, columns], preferred_element_type=f32)
        total = jnp.sum(mixed * depth_ref[:, columns], axis=0, keepdims=True)
        for k in range(8):
            sum_ref[pl.ds(64 * c + 8 * t + k, 1), :] = total[:, 128 * k : 128 * k + 128]
        return 0

    lax.fori_loop(0, SLOTS // 1024, some, 0)


def step_kernel(payload_ref, velocity_ref, next_ref, back_ref, *scratch):
    (
        mid_ref, recv_ref, values_ref, wts_ref, cell_ref, plane_ref, push_ref, depth_ref, field_ref,
        v1_ref, v2_ref, across_ref, sum_ref, send_ref, middle_ref,
    ) = scratch[:15]
    strips, got, sems = scratch[15:23], scratch[23:31], scratch[31:]
    ahead = (sems[0:2], sems[2:4])
    behind = (sems[4:6], sems[6:8])
    around, here = sems[8:10], sems[10]
    gx, gy = lax.axis_index("gx"), lax.axis_index("gy")
    sides = [(lax.rem(gx + dx + GX, GX), lax.rem(gy + dy + GY, GY)) for dx, dy in SIDES]
    peers = [(lax.rem(gx + k, GX), gy) for k in range(1, GX)] + [(gx, lax.rem(gy + k, GY)) for k in range(1, GY)]
    peers = peers + sides[4:]
    barrier = pltpu.get_barrier_semaphore()
    for peer in peers:
        pl.semaphore_signal(barrier, inc=1, device_id=peer, device_id_type=MESH)
    pl.semaphore_wait(barrier, len(peers))

    two_stage("gx", GX, "gy", GY, payload_ref, mid_ref, recv_ref, *ahead, here.at[0:2])
    received = recv_ref[...].reshape(DEVICES, 4, 128)
    for pair in range(3):
        values_ref[128 * pair : 128 * pair + 128, :] = received[:, pair, :].T
    weights(values_ref, wts_ref, cell_ref)
    fill_tables(values_ref, wts_ref, cell_ref, plane_ref, push_ref, depth_ref)
    v1_ref[0] = jnp.zeros((EXT, NZ), f32)
    v1_ref[EXT - 1] = jnp.zeros((EXT, NZ), f32)
    v2_ref[ROWS:, :] = jnp.zeros((PADDED - ROWS, NZ), f32)
    sum_ref[...] = jnp.zeros((256, 128), f32)
    copies = []

    def spread_and_send(c):
        spread(c, velocity_ref, plane_ref, push_ref, field_ref, strips)
        copies.append([send(strips[k].at[c], got[k].at[c], around, 8 * c + k, sides[k]) for k in range(8)])

    def receive_and_sweep(c):
        for copy in copies[c]:
            copy.wait_recv()
        sweep(c, field_ref, got, v1_ref, v2_ref, next_ref, across_ref)

    spread_and_send(0)
    spread_and_send(1)
    receive_and_sweep(0)
    spread_and_send(2)
    receive_and_sweep(1)
    interpolate(0, across_ref, plane_ref, depth_ref, sum_ref)
    receive_and_sweep(2)
    interpolate(1, across_ref, plane_ref, depth_ref, sum_ref)
    interpolate(2, across_ref, plane_ref, depth_ref, sum_ref)
    send_ref[...] = jnp.stack([sum_ref[0:128, :].T, sum_ref[128:256, :].T], axis=1).reshape(GY, GX, 2, 128)
    two_stage("gy", GY, "gx", GX, send_ref, middle_ref, back_ref, *behind, here.at[2:4])
    for some in copies:
        for copy in some:
            copy.wait_send()


def step(payload, velocity):
    dma = pltpu.SemaphoreType.DMA
    strips = [pltpu.VMEM((3, side_rows(side), NZ), bf16) for side in SIDES]
    return pl.pallas_call(
        step_kernel,
        out_shape=[
            jax.ShapeDtypeStruct((3 * CELLS, CELLS, NZ), f32),
            jax.ShapeDtypeStruct((GX, GY, 2, 128), f32),
        ],
        in_specs=[VMEM, VMEM],
        out_specs=[VMEM, VMEM],
        scratch_shapes=[
            pltpu.VMEM((GX, GY, 4, 128), f32),
            pltpu.VMEM((GY, GX, 4, 128), f32),
            pltpu.VMEM((384, 128), f32),
            pltpu.VMEM((12 * CAP, 128), f32),
            pltpu.VMEM((3 * CAP, 128), i32),
            pltpu.VMEM((PADDED, SLOTS), bf16),
            pltpu.VMEM((3, NZ, SLOTS), bf16),
            pltpu.VMEM((NZ, SLOTS), f32),
            pltpu.VMEM((3, EXT, EXT, NZ), f32),
            pltpu.VMEM((EXT, EXT, NZ), f32),
            pltpu.VMEM((PADDED, NZ), f32),
            pltpu.VMEM((3, NZ, PADDED), bf16),
            pltpu.VMEM((256, 128), f32),
            pltpu.VMEM((GY, GX, 2, 128), f32),
            pltpu.VMEM((GY, GX, 2, 128), f32),
            *strips,
            *strips,
            dma((GX,)), dma((GX,)), dma((GY,)), dma((GY,)),
            dma((GY,)), dma((GY,)), dma((GX,)), dma((GX,)),
            dma((24,)), dma((24,)), dma((4,)),
        ],
        compiler_params=params(61, collective_id=0, has_side_effects=True),
        cost_estimate=pl.CostEstimate(flops=4 * PADDED * SLOTS * 3 * NZ, bytes_accessed=10**7, transcendentals=0),
    )(payload, velocity)


def unpack_kernel(back_hbm, counts_hbm, out_ref, back_ref, counts_ref, sems, live_ref, flat_ref):
    fetch([(back_hbm, back_ref), (counts_hbm, counts_ref)], sems)
    live_ref[...] = counts_column(counts_ref)
    lane = lax.broadcasted_iota(i32, (16, 128), 1)
    for c in range(3):
        base = 64 * (c % 2)
        rows = [jnp.zeros((16, 128), f32)] * 3
        for j in range(8):
            row0, lane0 = divmod(CAP * j, 128)
            part = back_ref[pl.ds(2 * j + c // 2, 16, stride=16), :]
            part = jnp.where(lane - base < live_ref[pl.ds(j, 16, stride=8), :], part, 0.0)
            shift = (lane0 - base) % 128
            part = pltpu.roll(part, shift, 1) if shift else part
            rows[row0] = jnp.where((lane >= lane0) & (lane < lane0 + CAP), part, rows[row0])
            if lane0 + CAP > 128:
                rows[row0 + 1] = jnp.where(lane < lane0 + CAP - 128, part, rows[row0 + 1])
        for r in range(3):
            flat_ref[pl.ds(c * CAP + r, 16, stride=3), :] = rows[r]
        for r in range(CAP):
            out_ref[c : c + 1, 128 * r : 128 * r + 128] = flat_ref[c * CAP + r : c * CAP + r + 1, :]


def body(velocity, fiber_loads, fractions, corners, neighbours, counts):
    counts = counts.reshape(1, DEVICES)
    dma = pltpu.SemaphoreType.DMA
    payload = pl.pallas_call(
        prep_kernel,
        out_shape=jax.ShapeDtypeStruct((4 * DEVICES, 128), f32),
        in_specs=[ANY] * 5,
        out_specs=VMEM,
        scratch_shapes=[
            pltpu.VMEM((3, SLOTS), f32),
            pltpu.VMEM((3, SLOTS), f32),
            pltpu.VMEM((3, SLOTS), i32),
            pltpu.VMEM((CAP, 128), i32),
            pltpu.VMEM((1, DEVICES), i32),
            dma((5,)),
            pltpu.VMEM((DEVICES, DEVICES), i32),
            pltpu.VMEM((CAP, 128), f32),
            pltpu.VMEM((6 * CAP, 128), f32),
        ],
        compiler_params=params(),
    )(fiber_loads, fractions, corners, neighbours.reshape(CAP, 128), counts)
    mine = velocity.transpose(2, 0, 1, 3).reshape(3 * CELLS, CELLS, NZ)
    following, back = step(payload.reshape(GX, GY, 4, 128), mine)
    fiber_velocity = pl.pallas_call(
        unpack_kernel,
        out_shape=jax.ShapeDtypeStruct((3, SLOTS), f32),
        in_specs=[ANY] * 2,
        out_specs=VMEM,
        scratch_shapes=[
            pltpu.VMEM((2 * DEVICES, 128), f32),
            pltpu.VMEM((1, DEVICES), i32),
            dma((2,)),
            pltpu.VMEM((DEVICES, DEVICES), i32),
            pltpu.VMEM((3 * CAP, 128), f32),
        ],
        compiler_params=params(),
    )(back.reshape(2 * DEVICES, 128), counts)
    velocity_next = following.reshape(3, CELLS, CELLS, NZ).transpose(1, 2, 0, 3)
    return (velocity_next, fiber_velocity)


def solution(mesh):
    return jax.shard_map(
        body,
        mesh=mesh,
        in_specs=(
            P("gx", "gy", None, None),
            P(None, ("gx", "gy")),
            P(None, ("gx", "gy")),
            P(None, ("gx", "gy")),
            P(("gx", "gy")),
            P(("gx", "gy")),
        ),
        out_specs=(P("gx", "gy", None, None), P(None, ("gx", "gy"))),
        check_vma=False,
    )
```

```python
import functools

import jax
import jax.numpy as jnp
from jax import lax
from jax.experimental import pallas as pl
from jax.experimental.pallas import tpu as pltpu
from jax.sharding import PartitionSpec as P

viscosity = 0.15
GX, GY = 8, 16
DEVICES = GX * GY
CAP = 48
SLOTS = CAP * DEVICES
CELLS = 32
NZ = 256
EXT = 40
ROWS = 36 * EXT
PADDED = 1536
BLOCKS = CAP // 2
MESH = pl.DeviceIdType.MESH
VMEM = pl.BlockSpec(memory_space=pltpu.VMEM)
ANY = pl.BlockSpec(memory_space=pl.ANY)
f32, bf16, i32 = jnp.float32, jnp.bfloat16, jnp.int32


def params(mib=16, **more):
    return pltpu.CompilerParams(vmem_limit_bytes=mib * 2**20, **more)


def fetch(pairs, sems):
    copies = [pltpu.make_async_copy(src, dst, sems.at[k]) for k, (src, dst) in enumerate(pairs)]
    for copy in copies:
        copy.start()
    for copy in copies:
        copy.wait()


def counts_column(counts_ref):
    return jnp.broadcast_to(counts_ref[...].astype(f32), (DEVICES, DEVICES)).T.astype(i32)


def prepare(loads_ref, frac_ref, corner_ref, partner_ref, counts_ref, live_ref, flat_ref, pos_ref, out_ref):
    live_ref[...] = counts_column(counts_ref)

    def flat_rows(ref, c):
        for r in range(CAP):
            flat_ref[r : r + 1, :] = ref[c : c + 1, 128 * r : 128 * r + 128].astype(f32)
        return flat_ref[...]

    lane = lax.broadcasted_iota(i32, (CAP, 128), 1)
    flat_id = lax.broadcasted_iota(i32, (CAP, 128), 0) * 128 + lane
    bucket = (flat_id * 43691) >> 21
    partner = partner_ref[...]
    high, low = partner >> 7, partner & 127
    whole = (CELLS * GX, CELLS * GY, NZ)
    for c in range(3):
        fraction = flat_rows(frac_ref, c)
        corner = flat_rows(corner_ref, c)
        loads = flat_rows(loads_ref, c)
        position = corner + fraction
        flat_ref[...] = position
        gathered = jnp.zeros((CAP, 128), f32)
        for r in range(CAP):
            row = jnp.broadcast_to(flat_ref[r : r + 1, :], (CAP, 128))
            taken = jnp.take_along_axis(row, low, axis=1, mode="promise_in_bounds")
            gathered = jnp.where(high == r, taken, gathered)
        forcing = loads + (2.0 / whole[c]) * (gathered - position)
        pos_ref[c * CAP : c * CAP + CAP, :] = forcing
        cell = corner.astype(i32)
        if c == 0:
            cell = (cell - (bucket >> 4) * CELLS + 4) & (whole[0] - 1)
        if c == 1:
            cell = (cell - (bucket & 15) * CELLS + 4) & (whole[1] - 1)
        pos_ref[(3 + c) * CAP : (3 + c) * CAP + CAP, :] = cell.astype(f32) + fraction

    lane = lax.broadcasted_iota(i32, (8, 128), 1)
    for j in range(16):
        row0, lane0 = divmod(CAP * j, 128)
        live = (lane & 63) < live_ref[pl.ds(j, 8, stride=16), :]

        def piece(v, target):
            part = pos_ref[pl.ds(v * CAP + row0, 8, stride=6), :]
            if lane0 + CAP > 128:
                later = pos_ref[pl.ds(v * CAP + row0 + 1, 8, stride=6), :]
                part = jnp.where(lane >= lane0, part, later)
            shift = (target - lane0) % 128
            return pltpu.roll(part, shift, 1) if shift else part

        for pair in range(3):
            row = jnp.where(lane < 64, piece(2 * pair, 0), piece(2 * pair + 1, 64))
            if pair == 0:
                row = jnp.where(live, row, 0.0)
            if pair == 1:
                row = jnp.where(live | (lane >= 64), row, 0.0)
            out_ref[pl.ds(16 * pair + j, 8, stride=48), :] = row


def send(src, dst, sems, at, peer):
    copy = pltpu.make_async_remote_copy(
        src_ref=src,
        dst_ref=dst,
        send_sem=sems[0].at[at],
        recv_sem=sems[1].at[at],
        device_id=peer,
        device_id_type=MESH,
    )
    copy.start()
    return copy


def first_stage(axis, count, x_ref, mid_ref, sems, here):
    me = lax.axis_index(axis)
    own = pltpu.make_async_copy(x_ref.at[me], mid_ref.at[me], here)
    copies = []
    for k in range(1, count):
        peer = lax.rem(me + k, count)
        copies.append(send(x_ref.at[peer], mid_ref.at[me], sems, k, {axis: peer}))
    own.start()
    return [own], copies


def received(stage):
    own, copies = stage
    own[0].wait()
    for copy in copies:
        copy.wait_recv()


def sent(stage):
    for copy in stage[1]:
        copy.wait_send()


SIDES = ((-1, 0), (1, 0), (0, -1), (0, 1), (-1, -1), (-1, 1), (1, -1), (1, 1))
LOW, HIGH = (2, 8), (32, 38)


def side_rows(side):
    dx, dy = side
    return 6 * EXT if dy == 0 else 36 * 8 if dx == 0 else 6 * 8


def point_row(ref, base, block):
    return jnp.concatenate([ref[pl.ds(base + 2 * block, 1), :], ref[pl.ds(base + 2 * block + 1, 1), :]], axis=1)


def table(wts_ref, cell_ref, dim, block, length):
    corner = point_row(cell_ref, dim * CAP, block)
    delta = lax.broadcasted_iota(i32, (length, 256), 0) - corner
    if dim == 2:
        delta = delta & (NZ - 1)
    result = jnp.zeros((length, 256), f32)
    for k in range(4):
        result = jnp.where(delta == k, point_row(wts_ref, (4 * dim + k) * CAP, block), result)
    return result


def weights(values_ref, wts_ref, cell_ref):
    for dim in range(3):
        position = values_ref[64 * (3 + dim) : 64 * (3 + dim) + CAP, :]
        corner = jnp.floor(position)
        angle = (0.5 * jnp.pi) * (position - corner)
        sine, cosine = jnp.sin(angle), jnp.cos(angle)
        cell_ref[dim * CAP : dim * CAP + CAP, :] = corner.astype(i32)
        for k, term in enumerate((-sine, cosine, sine, -cosine)):
            at = (4 * dim + k) * CAP
            wts_ref[at : at + CAP, :] = 0.25 * (1.0 + term)


def fill_tables(values_ref, wts_ref, cell_ref, plane_ref, push_ref, depth_ref):
    def fill(block, _):
        columns = pl.ds(pl.multiple_of(block * 256, 256), 256)
        along_x = table(wts_ref, cell_ref, 0, block, EXT)
        along_y = table(wts_ref, cell_ref, 1, block, EXT)
        for i in range(18):
            x = 2 + 2 * i
            both = jnp.concatenate([along_y * along_x[x : x + 1], along_y * along_x[x + 1 : x + 2]], axis=0)
            plane_ref[80 * i : 80 * i + 80, columns] = both.astype(bf16)
        depth = table(wts_ref, cell_ref, 2, block, NZ)
        depth_ref[:, columns] = depth
        for c in range(3):
            push_ref[c, :, columns] = (depth * point_row(values_ref, 64 * c, block)).astype(bf16)
        return 0

    lax.fori_loop(0, BLOCKS, fill, 0)


def laplace(ref, x):
    center = ref[x]
    around = ref[x - 1] + ref[x + 1]
    around = around + pltpu.roll(center, 1, 0) + pltpu.roll(center, EXT - 1, 0)
    around = around + pltpu.roll(center, 1, 1) + pltpu.roll(center, NZ - 1, 1)
    return (1.0 - 6.0 * viscosity) * center + viscosity * around


def place_velocity(velocity_ref, field_ref):
    def place(t, _):
        for k in range(4):
            x = 4 * t + k
            for c in range(3):
                field_ref[c, x] = jnp.zeros((EXT, NZ), f32)
        return 0

    lax.fori_loop(0, EXT // 4, place, 0)

    def own(t, _):
        for k in range(4):
            x = 4 * t + k
            for c in range(3):
                field_ref[c, 4 + x, 4:36, :] = velocity_ref[x, c]
        return 0

    lax.fori_loop(0, CELLS // 4, own, 0)


def side_range(side):
    dx, dy = side
    first, last = (2, 38) if dx == 0 else LOW if dx < 0 else HIGH
    low, high = (0, EXT) if dy == 0 else (0, 8) if dy < 0 else (32, 40)
    return first, last, low, high


def opposite_range(side):
    dx, dy = side
    first, last = (2, 38) if dx == 0 else (34, 40) if dx < 0 else (0, 6)
    low, high = (0, EXT) if dy == 0 else (32, 40) if dy < 0 else (0, 8)
    return first, last, low, high


def pass_over(tasks):
    def some(t, _):
        for task in tasks:
            task(t)
        return 0

    lax.fori_loop(0, 6, some, 0)


def step_kernel(*refs):
    inputs, velocity_hbm = refs[:5], refs[5]
    next_hbm, back_ref = refs[6:8]
    scratch = refs[8:]
    staged, fetch_sems, (live_ref, flat_ref, pos_ref, payload_ref) = scratch[:5], scratch[5], scratch[6:10]
    mid_ref, turned_ref, recv_ref, values_ref, wts_ref, cell_ref = scratch[10:16]
    plane_ref, push_ref, depth_ref, field_ref, v1_ref, v2_ref, across_ref = scratch[16:23]
    sum_ref, out_ref, middle_ref, about_ref, velocity_ref, next_ref = scratch[23:29]
    strips, got, sems = scratch[29:37], scratch[37:45], scratch[45:]
    ahead, behind, around = (sems[0:2], sems[2:4]), (sems[4:6], sems[6:8], sems[8:10], sems[10:12]), sems[12:14]
    here, bulk = sems[14], sems[15]

    gx, gy = lax.axis_index("gx"), lax.axis_index("gy")
    sides = [(lax.rem(gx + dx + GX, GX), lax.rem(gy + dy + GY, GY)) for dx, dy in SIDES]
    peers = [(lax.rem(gx + k, GX), gy) for k in range(1, GX)] + [(gx, lax.rem(gy + k, GY)) for k in range(1, GY)]
    peers = peers + sides[4:]
    barrier = pltpu.get_barrier_semaphore()
    for peer in peers:
        pl.semaphore_signal(barrier, inc=1, device_id=peer, device_id_type=MESH)
    fetch(list(zip(inputs, staged)), fetch_sems)
    own_velocity = pltpu.make_async_copy(velocity_hbm, velocity_ref, bulk.at[3])
    own_velocity.start()
    prepare(*staged, live_ref, flat_ref, pos_ref, payload_ref)
    pl.semaphore_wait(barrier, len(peers))

    stage1 = first_stage("gx", GX, payload_ref.reshape(GX, 48, 128), mid_ref, ahead[0], here.at[0])
    own_velocity.wait()
    place_velocity(velocity_ref, field_ref)
    received(stage1)
    for a in range(GX):
        for pair in range(3):
            turned_ref[pl.ds(8 * pair + a, GY, stride=24), :] = mid_ref[a, 16 * pair : 16 * pair + 16, :]
    stage2 = first_stage("gy", GY, turned_ref.reshape(GY, 24, 128), recv_ref, ahead[1], here.at[1])
    plane_ref[ROWS:, :] = jnp.zeros((PADDED - ROWS, SLOTS), bf16)
    v2_ref[ROWS:, :] = jnp.zeros((PADDED - ROWS, NZ), f32)
    sum_ref[...] = jnp.zeros((256, 128), f32)
    received(stage2)
    for pair in range(3):
        values_ref[128 * pair : 128 * pair + 128, :] = recv_ref[:, 8 * pair : 8 * pair + 8, :].reshape(DEVICES, 128).T
    weights(values_ref, wts_ref, cell_ref)
    fill_tables(values_ref, wts_ref, cell_ref, plane_ref, push_ref, depth_ref)

    def spread(c):
        def some(t):
            part = lax.dot_general(
                plane_ref[pl.ds(pl.multiple_of(240 * t, 240), 240), :],
                push_ref[c],
                (((1,), (1,)), ((), ())),
                preferred_element_type=f32,
            )
            field_ref[c, pl.ds(2 + 6 * t, 6)] += part.reshape(6, EXT, NZ)

        return some

    def sweep(c):
        field = field_ref.at[c]

        def some(t):
            for k in range(6):
                x = 3 + 6 * t + k
                v1_ref[x] = laplace(field, x)
            for k in range(6):
                x = 6 * t + k
                value = laplace(v1_ref, x + 2)
                v2_ref[pl.ds(pl.multiple_of(x * EXT, 8), EXT), :] = value
                next_ref[x, c] = value[4:36]

        return some

    def interpolate(c):
        def some(t):
            columns = pl.ds(pl.multiple_of(t * 1024, 1024), 1024)
            mixed = jnp.dot(across_ref[c], plane_ref[:, columns], preferred_element_type=f32)
            total = jnp.sum(mixed * depth_ref[:, columns], axis=0, keepdims=True)
            for k in range(8):
                sum_ref[pl.ds(64 * c + 8 * t + k, 1), :] = total[:, 128 * k : 128 * k + 128]

        return some

    halos = []

    def send_halo(c):
        copies = []
        for k, side in enumerate(SIDES):
            first, last, low, high = side_range(side)
            strips[k][c] = field_ref[c, first:last, low:high, :].reshape(side_rows(side), NZ).astype(bf16)
            copies.append(send(strips[k].at[c], got[k].at[c], around, 8 * c + k, sides[k]))
        halos.append(copies)

    def receive_halo(c):
        for copy in halos[c]:
            copy.wait_recv()
        for side, strip in zip(SIDES, got):
            first, last, low, high = opposite_range(side)
            part = strip[c].astype(f32).reshape(last - first, high - low, NZ)
            field_ref[c, first:last, low:high, :] += part
        for x in (1, 2):
            v1_ref[x] = laplace(field_ref.at[c], x)

    def turn_over(c):
        for part in range(PADDED // 128):
            piece = v2_ref[128 * part : 128 * part + 128, :]
            across_ref[c, :, 128 * part : 128 * part + 128] = piece.T.astype(bf16)

    pass_over([spread(0)])
    send_halo(0)
    pass_over([spread(1)])
    send_halo(1)
    receive_halo(0)
    pass_over([spread(2), sweep(0)])
    send_halo(2)
    turn_over(0)
    receive_halo(1)
    pass_over([interpolate(0), sweep(1)])
    turn_over(1)
    receive_halo(2)
    pass_over([interpolate(1), sweep(2)])
    turn_over(2)
    own_next = pltpu.make_async_copy(next_ref.at[2:34], next_hbm, bulk.at[2])
    own_next.start()

    def depart(h):
        out_ref[h] = sum_ref[128 * h : 128 * h + 128, :].T.reshape(GY, GX, 128)
        return first_stage("gy", GY, out_ref.at[h], middle_ref.at[h], behind[2 * h], here.at[2 + h])

    def forward(h):
        for b in range(GY):
            about_ref[h, pl.ds(b, GX, stride=GY), :] = middle_ref[h, b]
        turned = about_ref.at[h].reshape(GX, GY, 128)
        return first_stage("gx", GX, turned, back_ref.at[h], behind[2 * h + 1], bulk.at[h])

    def half(first):
        def some(t, _):
            interpolate(2)(t)
            return 0

        lax.fori_loop(first, first + 3, some, 0)

    back = [depart(0)]
    half(0)
    received(back[0])
    back.append(forward(0))
    half(3)
    back.append(depart(1))
    received(back[2])
    back.append(forward(1))
    received(back[1])
    received(back[3])
    own_next.wait()
    for stage in [stage1, stage2] + back:
        sent(stage)
    for copies in halos:
        for copy in copies:
            copy.wait_send()


def step(inputs, velocity):
    dma = pltpu.SemaphoreType.DMA
    strips = [pltpu.VMEM((3, side_rows(side), NZ), bf16) for side in SIDES]
    return pl.pallas_call(
        step_kernel,
        out_shape=[
            jax.ShapeDtypeStruct((CELLS, 3, CELLS, NZ), f32),
            jax.ShapeDtypeStruct((2, GX, GY, 128), f32),
        ],
        in_specs=[ANY] * 6,
        out_specs=[ANY, VMEM],
        scratch_shapes=[
            pltpu.VMEM((3, SLOTS), f32),
            pltpu.VMEM((3, SLOTS), f32),
            pltpu.VMEM((3, SLOTS), i32),
            pltpu.VMEM((CAP, 128), i32),
            pltpu.VMEM((1, DEVICES), i32),
            dma((5,)),
            pltpu.VMEM((DEVICES, DEVICES), i32),
            pltpu.VMEM((CAP, 128), f32),
            pltpu.VMEM((6 * CAP, 128), f32),
            pltpu.VMEM((GX * 48, 128), f32),
            pltpu.VMEM((GX, 48, 128), f32),
            pltpu.VMEM((GY * 24, 128), f32),
            pltpu.VMEM((GY, 24, 128), f32),
            pltpu.VMEM((384, 128), f32),
            pltpu.VMEM((12 * CAP, 128), f32),
            pltpu.VMEM((3 * CAP, 128), i32),
            pltpu.VMEM((PADDED, SLOTS), bf16),
            pltpu.VMEM((3, NZ, SLOTS), bf16),
            pltpu.VMEM((NZ, SLOTS), f32),
            pltpu.VMEM((3, EXT, EXT, NZ), f32),
            pltpu.VMEM((EXT, EXT, NZ), f32),
            pltpu.VMEM((PADDED, NZ), f32),
            pltpu.VMEM((3, NZ, PADDED), bf16),
            pltpu.VMEM((256, 128), f32),
            pltpu.VMEM((2, GY, GX, 128), f32),
            pltpu.VMEM((2, GY, GX, 128), f32),
            pltpu.VMEM((2, DEVICES, 128), f32),
            pltpu.VMEM((CELLS, 3, CELLS, NZ), f32),
            pltpu.VMEM((CELLS + 4, 3, CELLS, NZ), f32),
            *strips,
            *strips,
            dma((GX,)), dma((GX,)), dma((GY,)), dma((GY,)),
            dma((GY,)), dma((GY,)), dma((GX,)), dma((GX,)),
            dma((GY,)), dma((GY,)), dma((GX,)), dma((GX,)),
            dma((24,)), dma((24,)), dma((4,)), dma((4,)),
        ],
        compiler_params=params(61, collective_id=0, has_side_effects=True),
        cost_estimate=pl.CostEstimate(flops=4 * PADDED * SLOTS * 3 * NZ, bytes_accessed=10**7, transcendentals=0),
    )(*inputs, velocity)


def unpack_kernel(back_hbm, counts_hbm, out_ref, back_ref, counts_ref, sems, live_ref, flat_ref):
    fetch([(back_hbm, back_ref), (counts_hbm, counts_ref)], sems)
    live_ref[...] = counts_column(counts_ref)
    lane = lax.broadcasted_iota(i32, (16, 128), 1)
    for c in range(3):
        base = 64 * (c % 2)
        rows = [jnp.zeros((16, 128), f32)] * 3
        for j in range(8):
            row0, lane0 = divmod(CAP * j, 128)
            part = back_ref[pl.ds(DEVICES * (c // 2) + j, 16, stride=8), :]
            part = jnp.where(lane - base < live_ref[pl.ds(j, 16, stride=8), :], part, 0.0)
            shift = (lane0 - base) % 128
            part = pltpu.roll(part, shift, 1) if shift else part
            rows[row0] = jnp.where((lane >= lane0) & (lane < lane0 + CAP), part, rows[row0])
            if lane0 + CAP > 128:
                rows[row0 + 1] = jnp.where(lane < lane0 + CAP - 128, part, rows[row0 + 1])
        for r in range(3):
            flat_ref[pl.ds(c * CAP + r, 16, stride=3), :] = rows[r]
        for r in range(CAP):
            out_ref[c : c + 1, 128 * r : 128 * r + 128] = flat_ref[c * CAP + r : c * CAP + r + 1, :]


def body(velocity, fiber_loads, fractions, corners, neighbours, counts):
    counts = counts.reshape(1, DEVICES)
    dma = pltpu.SemaphoreType.DMA
    inputs = (fiber_loads, fractions, corners, neighbours.reshape(CAP, 128), counts)
    following, back = step(inputs, velocity.transpose(0, 2, 1, 3))
    fiber_velocity = pl.pallas_call(
        unpack_kernel,
        out_shape=jax.ShapeDtypeStruct((3, SLOTS), f32),
        in_specs=[ANY] * 2,
        out_specs=VMEM,
        scratch_shapes=[
            pltpu.VMEM((2 * DEVICES, 128), f32),
            pltpu.VMEM((1, DEVICES), i32),
            dma((2,)),
            pltpu.VMEM((DEVICES, DEVICES), i32),
            pltpu.VMEM((3 * CAP, 128), f32),
        ],
        compiler_params=params(),
    )(back.reshape(2 * DEVICES, 128), counts)
    velocity_next = following.transpose(0, 2, 1, 3)
    return (velocity_next, fiber_velocity)


def solution(mesh):
    return jax.shard_map(
        body,
        mesh=mesh,
        in_specs=(
            P("gx", "gy", None, None),
            P(None, ("gx", "gy")),
            P(None, ("gx", "gy")),
            P(None, ("gx", "gy")),
            P(("gx", "gy")),
            P(("gx", "gy")),
        ),
        out_specs=(P("gx", "gy", None, None), P(None, ("gx", "gy"))),
        check_vma=False,
    )
```

```python
import functools

import jax
import jax.numpy as jnp
from jax import lax
from jax.experimental import pallas as pl
from jax.experimental.pallas import tpu as pltpu
from jax.sharding import PartitionSpec as P

viscosity = 0.15
GX, GY = 8, 16
DEVICES = GX * GY
CAP = 48
SLOTS = CAP * DEVICES
CELLS = 32
NZ = 256
EXT = 40
ROWS = 36 * EXT
PADDED = 1536
BLOCKS = CAP // 2
MESH = pl.DeviceIdType.MESH
VMEM = pl.BlockSpec(memory_space=pltpu.VMEM)
ANY = pl.BlockSpec(memory_space=pl.ANY)
HBM = pl.BlockSpec(memory_space=pltpu.MemorySpace.HBM)
f32, bf16, i32 = jnp.float32, jnp.bfloat16, jnp.int32


def params(mib=16, **more):
    return pltpu.CompilerParams(vmem_limit_bytes=mib * 2**20, **more)


def fetch(pairs, sems):
    copies = [pltpu.make_async_copy(src, dst, sems.at[k]) for k, (src, dst) in enumerate(pairs)]
    for copy in copies:
        copy.start()
    for copy in copies:
        copy.wait()


def counts_column(counts_ref):
    return jnp.broadcast_to(counts_ref[...].astype(f32), (DEVICES, DEVICES)).T.astype(i32)


def prepare(loads_ref, frac_ref, corner_ref, partner_ref, counts_ref, live_ref, flat_ref, pos_ref, out_ref):
    live_ref[...] = counts_column(counts_ref)

    def flat_rows(ref, c):
        for r in range(CAP):
            flat_ref[r : r + 1, :] = ref[c : c + 1, 128 * r : 128 * r + 128].astype(f32)
        return flat_ref[...]

    lane = lax.broadcasted_iota(i32, (CAP, 128), 1)
    flat_id = lax.broadcasted_iota(i32, (CAP, 128), 0) * 128 + lane
    bucket = (flat_id * 43691) >> 21
    partner = partner_ref[...]
    high, low = partner >> 7, partner & 127
    whole = (CELLS * GX, CELLS * GY, NZ)
    for c in range(3):
        fraction = flat_rows(frac_ref, c)
        corner = flat_rows(corner_ref, c)
        loads = flat_rows(loads_ref, c)
        position = corner + fraction
        flat_ref[...] = position
        gathered = jnp.zeros((CAP, 128), f32)
        for r in range(CAP):
            row = jnp.broadcast_to(flat_ref[r : r + 1, :], (CAP, 128))
            taken = jnp.take_along_axis(row, low, axis=1, mode="promise_in_bounds")
            gathered = jnp.where(high == r, taken, gathered)
        forcing = loads + (2.0 / whole[c]) * (gathered - position)
        pos_ref[c * CAP : c * CAP + CAP, :] = forcing
        cell = corner.astype(i32)
        if c == 0:
            cell = (cell - (bucket >> 4) * CELLS + 4) & (whole[0] - 1)
        if c == 1:
            cell = (cell - (bucket & 15) * CELLS + 4) & (whole[1] - 1)
        pos_ref[(3 + c) * CAP : (3 + c) * CAP + CAP, :] = cell.astype(f32) + fraction

    lane = lax.broadcasted_iota(i32, (8, 128), 1)
    for j in range(16):
        row0, lane0 = divmod(CAP * j, 128)
        live = (lane & 63) < live_ref[pl.ds(j, 8, stride=16), :]

        def piece(v, target):
            part = pos_ref[pl.ds(v * CAP + row0, 8, stride=6), :]
            if lane0 + CAP > 128:
                later = pos_ref[pl.ds(v * CAP + row0 + 1, 8, stride=6), :]
                part = jnp.where(lane >= lane0, part, later)
            shift = (target - lane0) % 128
            return pltpu.roll(part, shift, 1) if shift else part

        for pair in range(3):
            row = jnp.where(lane < 64, piece(2 * pair, 0), piece(2 * pair + 1, 64))
            if pair == 0:
                row = jnp.where(live, row, 0.0)
            if pair == 1:
                row = jnp.where(live | (lane >= 64), row, 0.0)
            out_ref[pl.ds(16 * pair + j, 8, stride=48), :] = row


def send(src, dst, sems, at, peer):
    copy = pltpu.make_async_remote_copy(
        src_ref=src,
        dst_ref=dst,
        send_sem=sems[0].at[at],
        recv_sem=sems[1].at[at],
        device_id=peer,
        device_id_type=MESH,
    )
    copy.start()
    return copy


def first_stage(axis, count, x_ref, mid_ref, sems, here):
    me = lax.axis_index(axis)
    own = pltpu.make_async_copy(x_ref.at[me], mid_ref.at[me], here)
    copies = []
    for k in range(1, count):
        peer = lax.rem(me + k, count)
        copies.append(send(x_ref.at[peer], mid_ref.at[me], sems, k, {axis: peer}))
    own.start()
    return [own], copies


def received(stage):
    own, copies = stage
    own[0].wait()
    for copy in copies:
        copy.wait_recv()


def sent(stage):
    for copy in stage[1]:
        copy.wait_send()


SIDES = ((-1, 0), (1, 0), (0, -1), (0, 1), (-1, -1), (-1, 1), (1, -1), (1, 1))
LOW, HIGH = (2, 8), (32, 38)


def side_rows(side):
    dx, dy = side
    return 6 * EXT if dy == 0 else 36 * 8 if dx == 0 else 6 * 8


def point_row(ref, base, block):
    return jnp.concatenate([ref[pl.ds(base + 2 * block, 1), :], ref[pl.ds(base + 2 * block + 1, 1), :]], axis=1)


def table(wts_ref, cell_ref, dim, block, length):
    corner = point_row(cell_ref, dim * CAP, block)
    delta = lax.broadcasted_iota(i32, (length, 256), 0) - corner
    if dim == 2:
        delta = delta & (NZ - 1)
    result = jnp.zeros((length, 256), f32)
    for k in range(4):
        result = jnp.where(delta == k, point_row(wts_ref, (4 * dim + k) * CAP, block), result)
    return result


def weights(values_ref, wts_ref, cell_ref):
    for dim in range(3):
        position = values_ref[64 * (3 + dim) : 64 * (3 + dim) + CAP, :]
        corner = jnp.floor(position)
        angle = (0.5 * jnp.pi) * (position - corner)
        sine, cosine = jnp.sin(angle), jnp.cos(angle)
        cell_ref[dim * CAP : dim * CAP + CAP, :] = corner.astype(i32)
        for k, term in enumerate((-sine, cosine, sine, -cosine)):
            at = (4 * dim + k) * CAP
            wts_ref[at : at + CAP, :] = 0.25 * (1.0 + term)


def fill_tables(values_ref, wts_ref, cell_ref, plane_ref, push_ref, depth_ref):
    def fill(block, _):
        columns = pl.ds(pl.multiple_of(block * 256, 256), 256)
        along_x = table(wts_ref, cell_ref, 0, block, EXT)
        along_y = table(wts_ref, cell_ref, 1, block, EXT)
        for i in range(18):
            x = 2 + 2 * i
            both = jnp.concatenate([along_y * along_x[x : x + 1], along_y * along_x[x + 1 : x + 2]], axis=0)
            plane_ref[80 * i : 80 * i + 80, columns] = both.astype(bf16)
        depth = table(wts_ref, cell_ref, 2, block, NZ)
        depth_ref[:, columns] = depth
        for c in range(3):
            push_ref[c, :, columns] = (depth * point_row(values_ref, 64 * c, block)).astype(bf16)
        return 0

    lax.fori_loop(0, BLOCKS, fill, 0)


def laplace(ref, x):
    center = ref[x]
    around = ref[x - 1] + ref[x + 1]
    around = around + pltpu.roll(center, 1, 0) + pltpu.roll(center, EXT - 1, 0)
    around = around + pltpu.roll(center, 1, 1) + pltpu.roll(center, NZ - 1, 1)
    return (1.0 - 6.0 * viscosity) * center + viscosity * around


def place_velocity(velocity_ref, field_ref):
    def place(t, _):
        for k in range(4):
            x = 4 * t + k
            for c in range(3):
                field_ref[c, x] = jnp.zeros((EXT, NZ), f32)
        return 0

    lax.fori_loop(0, EXT // 4, place, 0)

    def own(t, _):
        for k in range(4):
            x = 4 * t + k
            for c in range(3):
                field_ref[c, 4 + x, 4:36, :] = velocity_ref[x, c]
        return 0

    lax.fori_loop(0, CELLS // 4, own, 0)


def side_range(side):
    dx, dy = side
    first, last = (2, 38) if dx == 0 else LOW if dx < 0 else HIGH
    low, high = (0, EXT) if dy == 0 else (0, 8) if dy < 0 else (32, 40)
    return first, last, low, high


def opposite_range(side):
    dx, dy = side
    first, last = (2, 38) if dx == 0 else (34, 40) if dx < 0 else (0, 6)
    low, high = (0, EXT) if dy == 0 else (32, 40) if dy < 0 else (0, 8)
    return first, last, low, high


def pass_over(steps, tasks):
    def some(t, _):
        for task in tasks:
            task(t)
        return 0

    lax.fori_loop(0, steps, some, 0, unroll=True)


def step_kernel(*refs):
    inputs, velocity_hbm = refs[:5], refs[5]
    next_hbm, back_ref = refs[6:8]
    scratch = refs[8:]
    staged, fetch_sems, (live_ref, flat_ref, pos_ref, payload_ref) = scratch[:5], scratch[5], scratch[6:10]
    mid_ref, turned_ref, recv_ref, values_ref, wts_ref, cell_ref = scratch[10:16]
    plane_ref, push_ref, depth_ref, field_ref, v1_ref, v2_ref, across_ref = scratch[16:23]
    sum_ref, out_ref, middle_ref, about_ref, velocity_ref, next_ref = scratch[23:29]
    strips, got, sems = scratch[29:37], scratch[37:45], scratch[45:]
    ahead, behind, around = (sems[0:2], sems[2:4]), (sems[4:6], sems[6:8], sems[8:10], sems[10:12]), sems[12:14]
    here, bulk = sems[14], sems[15]

    gx, gy = lax.axis_index("gx"), lax.axis_index("gy")
    sides = [(lax.rem(gx + dx + GX, GX), lax.rem(gy + dy + GY, GY)) for dx, dy in SIDES]
    peers = [(lax.rem(gx + k, GX), gy) for k in range(1, GX)] + [(gx, lax.rem(gy + k, GY)) for k in range(1, GY)]
    peers = peers + sides[4:]
    barrier = pltpu.get_barrier_semaphore()
    for peer in peers:
        pl.semaphore_signal(barrier, inc=1, device_id=peer, device_id_type=MESH)
    fetch(list(zip(inputs, staged)), fetch_sems)
    own_velocity = pltpu.make_async_copy(velocity_hbm, velocity_ref, bulk.at[3])
    own_velocity.start()
    prepare(*staged, live_ref, flat_ref, pos_ref, payload_ref)
    pl.semaphore_wait(barrier, len(peers))

    stage1 = first_stage("gx", GX, payload_ref.reshape(GX, 48, 128), mid_ref, ahead[0], here.at[0])
    own_velocity.wait()
    place_velocity(velocity_ref, field_ref)
    received(stage1)
    for a in range(GX):
        for pair in range(3):
            turned_ref[pl.ds(8 * pair + a, GY, stride=24), :] = mid_ref[a, 16 * pair : 16 * pair + 16, :]
    stage2 = first_stage("gy", GY, turned_ref.reshape(GY, 24, 128), recv_ref, ahead[1], here.at[1])
    plane_ref[ROWS:, :] = jnp.zeros((PADDED - ROWS, SLOTS), bf16)
    v2_ref[ROWS:, :] = jnp.zeros((PADDED - ROWS, NZ), f32)
    sum_ref[...] = jnp.zeros((256, 128), f32)
    received(stage2)
    for pair in range(3):
        values_ref[128 * pair : 128 * pair + 128, :] = recv_ref[:, 8 * pair : 8 * pair + 8, :].reshape(DEVICES, 128).T
    weights(values_ref, wts_ref, cell_ref)
    fill_tables(values_ref, wts_ref, cell_ref, plane_ref, push_ref, depth_ref)

    def spread(c):
        def some(t):
            part = lax.dot_general(
                plane_ref[pl.ds(pl.multiple_of(720 * t, 720), 720), :],
                push_ref[c],
                (((1,), (1,)), ((), ())),
                preferred_element_type=f32,
            )
            field_ref[c, pl.ds(2 + 18 * t, 18)] += part.reshape(18, EXT, NZ)

        return some

    def sweep(c, count):
        field = field_ref.at[c]

        def some(t):
            for k in range(count):
                x = 3 + count * t + k
                v1_ref[x] = laplace(field, x)
            for k in range(count):
                x = count * t + k
                value = laplace(v1_ref, x + 2)
                v2_ref[pl.ds(pl.multiple_of(x * EXT, 8), EXT), :] = value
                next_ref[x, c] = value[4:36]

        return some

    def interpolate(c):
        def some(t):
            columns = pl.ds(pl.multiple_of(t * 1024, 1024), 1024)
            mixed = jnp.dot(across_ref[c], plane_ref[:, columns], preferred_element_type=f32)
            total = jnp.sum(mixed * depth_ref[:, columns], axis=0, keepdims=True)
            for k in range(8):
                sum_ref[pl.ds(64 * c + 8 * t + k, 1), :] = total[:, 128 * k : 128 * k + 128]

        return some

    halos = []

    def send_halo(c):
        copies = []
        for k, side in enumerate(SIDES):
            first, last, low, high = side_range(side)
            strips[k][c] = field_ref[c, first:last, low:high, :].reshape(side_rows(side), NZ).astype(bf16)
            copies.append(send(strips[k].at[c], got[k].at[c], around, 8 * c + k, sides[k]))
        halos.append(copies)

    def receive_halo(c):
        for copy in halos[c]:
            copy.wait_recv()
        for side, strip in zip(SIDES, got):
            first, last, low, high = opposite_range(side)
            part = strip[c].astype(f32).reshape(last - first, high - low, NZ)
            field_ref[c, first:last, low:high, :] += part
        for x in (1, 2):
            v1_ref[x] = laplace(field_ref.at[c], x)

    def turn_over(c):
        for part in range(PADDED // 128):
            piece = v2_ref[128 * part : 128 * part + 128, :]
            across_ref[c, :, 128 * part : 128 * part + 128] = piece.T.astype(bf16)

    pass_over(2, [spread(0)])
    send_halo(0)
    pass_over(2, [spread(1)])
    send_halo(1)
    receive_halo(0)
    pass_over(2, [spread(2), sweep(0, 18)])
    send_halo(2)
    turn_over(0)
    receive_halo(1)
    pass_over(6, [interpolate(0), sweep(1, 6)])
    turn_over(1)
    receive_halo(2)
    pass_over(6, [interpolate(1), sweep(2, 6)])
    turn_over(2)
    own_next = pltpu.make_async_copy(next_ref.at[2:34], next_hbm, bulk.at[2])
    own_next.start()

    def depart(h):
        out_ref[h] = sum_ref[128 * h : 128 * h + 128, :].T.reshape(GY, GX, 128)
        return first_stage("gy", GY, out_ref.at[h], middle_ref.at[h], behind[2 * h], here.at[2 + h])

    def forward(h):
        for b in range(GY):
            about_ref[h, pl.ds(b, GX, stride=GY), :] = middle_ref[h, b]
        turned = about_ref.at[h].reshape(GX, GY, 128)
        return first_stage("gx", GX, turned, back_ref.at[h], behind[2 * h + 1], bulk.at[h])

    def half(first):
        def some(t, _):
            interpolate(2)(t)
            return 0

        lax.fori_loop(first, first + 3, some, 0, unroll=True)

    back = [depart(0)]
    half(0)
    received(back[0])
    back.append(forward(0))
    half(3)
    back.append(depart(1))
    received(back[2])
    back.append(forward(1))
    received(back[1])
    received(back[3])
    own_next.wait()
    for stage in [stage1, stage2] + back:
        sent(stage)
    for copies in halos:
        for copy in copies:
            copy.wait_send()


def step(inputs, velocity):
    dma = pltpu.SemaphoreType.DMA
    strips = [pltpu.VMEM((3, side_rows(side), NZ), bf16) for side in SIDES]
    return pl.pallas_call(
        step_kernel,
        out_shape=[
            jax.ShapeDtypeStruct((CELLS, 3, CELLS, NZ), f32),
            jax.ShapeDtypeStruct((2, GX, GY, 128), f32),
        ],
        in_specs=[ANY] * 6,
        out_specs=[ANY, VMEM],
        scratch_shapes=[
            pltpu.VMEM((3, SLOTS), f32),
            pltpu.VMEM((3, SLOTS), f32),
            pltpu.VMEM((3, SLOTS), i32),
            pltpu.VMEM((CAP, 128), i32),
            pltpu.VMEM((1, DEVICES), i32),
            dma((5,)),
            pltpu.VMEM((DEVICES, DEVICES), i32),
            pltpu.VMEM((CAP, 128), f32),
            pltpu.VMEM((6 * CAP, 128), f32),
            pltpu.VMEM((GX * 48, 128), f32),
            pltpu.VMEM((GX, 48, 128), f32),
            pltpu.VMEM((GY * 24, 128), f32),
            pltpu.VMEM((GY, 24, 128), f32),
            pltpu.VMEM((384, 128), f32),
            pltpu.VMEM((12 * CAP, 128), f32),
            pltpu.VMEM((3 * CAP, 128), i32),
            pltpu.VMEM((PADDED, SLOTS), bf16),
            pltpu.VMEM((3, NZ, SLOTS), bf16),
            pltpu.VMEM((NZ, SLOTS), f32),
            pltpu.VMEM((3, EXT, EXT, NZ), f32),
            pltpu.VMEM((EXT, EXT, NZ), f32),
            pltpu.VMEM((PADDED, NZ), f32),
            pltpu.VMEM((3, NZ, PADDED), bf16),
            pltpu.VMEM((256, 128), f32),
            pltpu.VMEM((2, GY, GX, 128), f32),
            pltpu.VMEM((2, GY, GX, 128), f32),
            pltpu.VMEM((2, DEVICES, 128), f32),
            pltpu.VMEM((CELLS, 3, CELLS, NZ), f32),
            pltpu.VMEM((CELLS + 4, 3, CELLS, NZ), f32),
            *strips,
            *strips,
            dma((GX,)), dma((GX,)), dma((GY,)), dma((GY,)),
            dma((GY,)), dma((GY,)), dma((GX,)), dma((GX,)),
            dma((GY,)), dma((GY,)), dma((GX,)), dma((GX,)),
            dma((24,)), dma((24,)), dma((4,)), dma((4,)),
        ],
        compiler_params=params(61, collective_id=0, has_side_effects=True),
        cost_estimate=pl.CostEstimate(flops=4 * PADDED * SLOTS * 3 * NZ, bytes_accessed=10**7, transcendentals=0),
    )(*inputs, velocity)


PIECES = 8


def unpack_kernel(back_hbm, counts_hbm, next_hbm, result_hbm, out_ref, *scratch):
    back_ref, counts_ref, sems, live_ref, flat_ref, next_ref, in_sems, out_sems = scratch
    size = CELLS // PIECES
    pieces = [pl.ds(size * k, size) for k in range(PIECES)]
    arrive = [pltpu.make_async_copy(next_hbm.at[p], next_ref.at[p], in_sems.at[k]) for k, p in enumerate(pieces)]
    leave = [pltpu.make_async_copy(next_ref.at[p], result_hbm.at[p], out_sems.at[k]) for k, p in enumerate(pieces)]
    small = [
        pltpu.make_async_copy(src, dst, sems.at[k])
        for k, (src, dst) in enumerate([(back_hbm, back_ref), (counts_hbm, counts_ref)])
    ]
    for copy in small + arrive:
        copy.start()
    for copy in small:
        copy.wait()
    for k in range(PIECES):
        arrive[k].wait()
        leave[k].start()
    live_ref[...] = counts_column(counts_ref)
    lane = lax.broadcasted_iota(i32, (16, 128), 1)
    for c in range(3):
        base = 64 * (c % 2)
        rows = [jnp.zeros((16, 128), f32)] * 3
        for j in range(8):
            row0, lane0 = divmod(CAP * j, 128)
            part = back_ref[pl.ds(DEVICES * (c // 2) + j, 16, stride=8), :]
            part = jnp.where(lane - base < live_ref[pl.ds(j, 16, stride=8), :], part, 0.0)
            shift = (lane0 - base) % 128
            part = pltpu.roll(part, shift, 1) if shift else part
            rows[row0] = jnp.where((lane >= lane0) & (lane < lane0 + CAP), part, rows[row0])
            if lane0 + CAP > 128:
                rows[row0 + 1] = jnp.where(lane < lane0 + CAP - 128, part, rows[row0 + 1])
        for r in range(3):
            flat_ref[pl.ds(c * CAP + r, 16, stride=3), :] = rows[r]
        for r in range(CAP):
            out_ref[c : c + 1, 128 * r : 128 * r + 128] = flat_ref[c * CAP + r : c * CAP + r + 1, :]
    for copy in leave:
        copy.wait()


def body(velocity, fiber_loads, fractions, corners, neighbours, counts):
    counts = counts.reshape(1, DEVICES)
    dma = pltpu.SemaphoreType.DMA
    inputs = (fiber_loads, fractions, corners, neighbours.reshape(CAP, 128), counts)
    following, back = step(inputs, velocity.transpose(0, 2, 1, 3))
    velocity_next, fiber_velocity = pl.pallas_call(
        unpack_kernel,
        out_shape=[
            jax.ShapeDtypeStruct((CELLS, 3, CELLS, NZ), f32),
            jax.ShapeDtypeStruct((3, SLOTS), f32),
        ],
        in_specs=[HBM] * 3,
        out_specs=[HBM, VMEM],
        scratch_shapes=[
            pltpu.VMEM((2 * DEVICES, 128), f32),
            pltpu.VMEM((1, DEVICES), i32),
            dma((2,)),
            pltpu.VMEM((DEVICES, DEVICES), i32),
            pltpu.VMEM((3 * CAP, 128), f32),
            pltpu.VMEM((CELLS, 3, CELLS, NZ), f32),
            dma((PIECES,)),
            dma((PIECES,)),
        ],
        compiler_params=params(61),
    )(back.reshape(2 * DEVICES, 128), counts, following)
    return (velocity_next.transpose(0, 2, 1, 3), fiber_velocity)


def solution(mesh):
    return jax.shard_map(
        body,
        mesh=mesh,
        in_specs=(
            P("gx", "gy", None, None),
            P(None, ("gx", "gy")),
            P(None, ("gx", "gy")),
            P(None, ("gx", "gy")),
            P(("gx", "gy")),
            P(("gx", "gy")),
        ),
        out_specs=(P("gx", "gy", None, None), P(None, ("gx", "gy"))),
        check_vma=False,
    )
```

```python
import functools

import jax
import jax.numpy as jnp
from jax import lax
from jax.experimental import pallas as pl
from jax.experimental.pallas import tpu as pltpu
from jax.sharding import PartitionSpec as P

viscosity = 0.15
GX, GY = 8, 16
DEVICES = GX * GY
CAP = 48
SLOTS = CAP * DEVICES
CELLS = 32
NZ = 256
EXT = 40
ROWS = 36 * EXT
PADDED = 1536
BLOCKS = CAP // 2
MESH = pl.DeviceIdType.MESH
VMEM = pl.BlockSpec(memory_space=pltpu.VMEM)
ANY = pl.BlockSpec(memory_space=pl.ANY)
HBM = pl.BlockSpec(memory_space=pltpu.MemorySpace.HBM)
f32, bf16, i32 = jnp.float32, jnp.bfloat16, jnp.int32


def params(mib=16, **more):
    return pltpu.CompilerParams(vmem_limit_bytes=mib * 2**20, **more)


def fetch(pairs, sems):
    copies = [pltpu.make_async_copy(src, dst, sems.at[k]) for k, (src, dst) in enumerate(pairs)]
    for copy in copies:
        copy.start()
    for copy in copies:
        copy.wait()


def counts_column(counts_ref):
    return jnp.broadcast_to(counts_ref[...].astype(f32), (DEVICES, DEVICES)).T.astype(i32)


def prepare(loads_ref, frac_ref, corner_ref, partner_ref, counts_ref, live_ref, flat_ref, pos_ref, out_ref):
    live_ref[...] = counts_column(counts_ref)

    def flat_rows(ref, c):
        for r in range(CAP):
            flat_ref[r : r + 1, :] = ref[c : c + 1, 128 * r : 128 * r + 128].astype(f32)
        return flat_ref[...]

    lane = lax.broadcasted_iota(i32, (CAP, 128), 1)
    flat_id = lax.broadcasted_iota(i32, (CAP, 128), 0) * 128 + lane
    bucket = (flat_id * 43691) >> 21
    partner = partner_ref[...]
    high, low = partner >> 7, partner & 127
    whole = (CELLS * GX, CELLS * GY, NZ)
    for c in range(3):
        fraction = flat_rows(frac_ref, c)
        corner = flat_rows(corner_ref, c)
        loads = flat_rows(loads_ref, c)
        position = corner + fraction
        flat_ref[...] = position
        gathered = jnp.zeros((CAP, 128), f32)
        for r in range(CAP):
            row = jnp.broadcast_to(flat_ref[r : r + 1, :], (CAP, 128))
            taken = jnp.take_along_axis(row, low, axis=1, mode="promise_in_bounds")
            gathered = jnp.where(high == r, taken, gathered)
        forcing = loads + (2.0 / whole[c]) * (gathered - position)
        pos_ref[c * CAP : c * CAP + CAP, :] = forcing
        cell = corner.astype(i32)
        if c == 0:
            cell = (cell - (bucket >> 4) * CELLS + 4) & (whole[0] - 1)
        if c == 1:
            cell = (cell - (bucket & 15) * CELLS + 4) & (whole[1] - 1)
        pos_ref[(3 + c) * CAP : (3 + c) * CAP + CAP, :] = cell.astype(f32) + fraction

    lane = lax.broadcasted_iota(i32, (8, 128), 1)
    for j in range(16):
        row0, lane0 = divmod(CAP * j, 128)
        live = (lane & 63) < live_ref[pl.ds(j, 8, stride=16), :]

        def piece(v, target):
            part = pos_ref[pl.ds(v * CAP + row0, 8, stride=6), :]
            if lane0 + CAP > 128:
                later = pos_ref[pl.ds(v * CAP + row0 + 1, 8, stride=6), :]
                part = jnp.where(lane >= lane0, part, later)
            shift = (target - lane0) % 128
            return pltpu.roll(part, shift, 1) if shift else part

        for pair in range(3):
            row = jnp.where(lane < 64, piece(2 * pair, 0), piece(2 * pair + 1, 64))
            if pair == 0:
                row = jnp.where(live, row, 0.0)
            if pair == 1:
                row = jnp.where(live | (lane >= 64), row, 0.0)
            out_ref[pl.ds(16 * pair + j, 8, stride=48), :] = row


def send(src, dst, sems, at, peer):
    copy = pltpu.make_async_remote_copy(
        src_ref=src,
        dst_ref=dst,
        send_sem=sems[0].at[at],
        recv_sem=sems[1].at[at],
        device_id=peer,
        device_id_type=MESH,
    )
    copy.start()
    return copy


def first_stage(axis, count, x_ref, mid_ref, sems, here):
    me = lax.axis_index(axis)
    own = pltpu.make_async_copy(x_ref.at[me], mid_ref.at[me], here)
    copies = []
    for k in range(1, count):
        peer = lax.rem(me + k, count)
        copies.append(send(x_ref.at[peer], mid_ref.at[me], sems, k, {axis: peer}))
    own.start()
    return [own], copies


def received(stage):
    own, copies = stage
    own[0].wait()
    for copy in copies:
        copy.wait_recv()


def sent(stage):
    for copy in stage[1]:
        copy.wait_send()


SIDES = ((-1, 0), (1, 0), (0, -1), (0, 1), (-1, -1), (-1, 1), (1, -1), (1, 1))
LOW, HIGH = (2, 8), (32, 38)


def side_rows(side):
    dx, dy = side
    return 6 * EXT if dy == 0 else 36 * 8 if dx == 0 else 6 * 8


def point_row(ref, base, block):
    return jnp.concatenate([ref[pl.ds(base + 2 * block, 1), :], ref[pl.ds(base + 2 * block + 1, 1), :]], axis=1)


def table(wts_ref, cell_ref, dim, block, length):
    corner = point_row(cell_ref, dim * CAP, block)
    delta = lax.broadcasted_iota(i32, (length, 256), 0) - corner
    if dim == 2:
        delta = delta & (NZ - 1)
    result = jnp.zeros((length, 256), f32)
    for k in range(4):
        result = jnp.where(delta == k, point_row(wts_ref, (4 * dim + k) * CAP, block), result)
    return result


def weights(values_ref, wts_ref, cell_ref):
    for dim in range(3):
        position = values_ref[64 * (3 + dim) : 64 * (3 + dim) + CAP, :]
        corner = jnp.floor(position)
        angle = (0.5 * jnp.pi) * (position - corner)
        sine, cosine = jnp.sin(angle), jnp.cos(angle)
        cell_ref[dim * CAP : dim * CAP + CAP, :] = corner.astype(i32)
        for k, term in enumerate((-sine, cosine, sine, -cosine)):
            at = (4 * dim + k) * CAP
            wts_ref[at : at + CAP, :] = 0.25 * (1.0 + term)


def fill_tables(values_ref, wts_ref, cell_ref, plane_ref, push_ref, depth_ref):
    def fill(block, _):
        columns = pl.ds(pl.multiple_of(block * 256, 256), 256)
        along_x = table(wts_ref, cell_ref, 0, block, EXT)
        along_y = table(wts_ref, cell_ref, 1, block, EXT)
        for i in range(18):
            x = 2 + 2 * i
            both = jnp.concatenate([along_y * along_x[x : x + 1], along_y * along_x[x + 1 : x + 2]], axis=0)
            plane_ref[80 * i : 80 * i + 80, columns] = both.astype(bf16)
        depth = table(wts_ref, cell_ref, 2, block, NZ)
        depth_ref[:, columns] = depth
        for c in range(3):
            push_ref[c, :, columns] = (depth * point_row(values_ref, 64 * c, block)).astype(bf16)
        return 0

    lax.fori_loop(0, BLOCKS, fill, 0)


def laplace(ref, x):
    center = ref[x]
    around = ref[x - 1] + ref[x + 1]
    around = around + pltpu.roll(center, 1, 0) + pltpu.roll(center, EXT - 1, 0)
    around = around + pltpu.roll(center, 1, 1) + pltpu.roll(center, NZ - 1, 1)
    return (1.0 - 6.0 * viscosity) * center + viscosity * around


def place_velocity(velocity_ref, field_ref):
    def place(t, _):
        for k in range(4):
            x = 4 * t + k
            for c in range(3):
                field_ref[c, x] = jnp.zeros((EXT, NZ), f32)
        return 0

    lax.fori_loop(0, EXT // 4, place, 0)

    def own(t, _):
        for k in range(4):
            x = 4 * t + k
            for c in range(3):
                field_ref[c, 4 + x, 4:36, :] = velocity_ref[x, c]
        return 0

    lax.fori_loop(0, CELLS // 4, own, 0)


def side_range(side):
    dx, dy = side
    first, last = (2, 38) if dx == 0 else LOW if dx < 0 else HIGH
    low, high = (0, EXT) if dy == 0 else (0, 8) if dy < 0 else (32, 40)
    return first, last, low, high


def opposite_range(side):
    dx, dy = side
    first, last = (2, 38) if dx == 0 else (34, 40) if dx < 0 else (0, 6)
    low, high = (0, EXT) if dy == 0 else (32, 40) if dy < 0 else (0, 8)
    return first, last, low, high


def pass_over(steps, tasks, unroll=False):
    def some(t, _):
        for task in tasks:
            task(t)
        return 0

    lax.fori_loop(0, steps, some, 0, unroll=unroll)


def step_kernel(*refs):
    inputs, velocity_hbm = refs[:5], refs[5]
    next_hbm, back_ref = refs[6:8]
    scratch = refs[8:]
    staged, fetch_sems, (live_ref, flat_ref, pos_ref, payload_ref) = scratch[:5], scratch[5], scratch[6:10]
    mid_ref, turned_ref, recv_ref, values_ref, wts_ref, cell_ref = scratch[10:16]
    plane_ref, push_ref, depth_ref, field_ref, v1_ref, v2_ref, across_ref = scratch[16:23]
    sum_ref, out_ref, middle_ref, about_ref, velocity_ref, next_ref = scratch[23:29]
    strips, got, sems = scratch[29:37], scratch[37:45], scratch[45:]
    ahead, behind, around = (sems[0:2], sems[2:4]), (sems[4:6], sems[6:8], sems[8:10]), sems[10:12]
    here, bulk = sems[12], sems[13]

    gx, gy = lax.axis_index("gx"), lax.axis_index("gy")
    sides = [(lax.rem(gx + dx + GX, GX), lax.rem(gy + dy + GY, GY)) for dx, dy in SIDES]
    peers = [(lax.rem(gx + k, GX), gy) for k in range(1, GX)] + [(gx, lax.rem(gy + k, GY)) for k in range(1, GY)]
    peers = peers + sides[4:]
    barrier = pltpu.get_barrier_semaphore()
    for peer in peers:
        pl.semaphore_signal(barrier, inc=1, device_id=peer, device_id_type=MESH)
    fetch(list(zip(inputs, staged)), fetch_sems)
    own_velocity = pltpu.make_async_copy(velocity_hbm, velocity_ref, bulk.at[3])
    own_velocity.start()
    prepare(*staged, live_ref, flat_ref, pos_ref, payload_ref)
    pl.semaphore_wait(barrier, len(peers))

    stage1 = first_stage("gx", GX, payload_ref.reshape(GX, 48, 128), mid_ref, ahead[0], here.at[0])
    own_velocity.wait()
    place_velocity(velocity_ref, field_ref)
    received(stage1)
    for a in range(GX):
        for pair in range(3):
            turned_ref[pl.ds(8 * pair + a, GY, stride=24), :] = mid_ref[a, 16 * pair : 16 * pair + 16, :]
    stage2 = first_stage("gy", GY, turned_ref.reshape(GY, 24, 128), recv_ref, ahead[1], here.at[1])
    plane_ref[ROWS:, :] = jnp.zeros((PADDED - ROWS, SLOTS), bf16)
    v2_ref[ROWS:, :] = jnp.zeros((PADDED - ROWS, NZ), f32)
    sum_ref[...] = jnp.zeros((256, 128), f32)
    received(stage2)
    for pair in range(3):
        values_ref[128 * pair : 128 * pair + 128, :] = recv_ref[:, 8 * pair : 8 * pair + 8, :].reshape(DEVICES, 128).T
    weights(values_ref, wts_ref, cell_ref)
    fill_tables(values_ref, wts_ref, cell_ref, plane_ref, push_ref, depth_ref)

    def spread(c):
        def some(t):
            part = lax.dot_general(
                plane_ref[pl.ds(pl.multiple_of(720 * t, 720), 720), :],
                push_ref[c],
                (((1,), (1,)), ((), ())),
                preferred_element_type=f32,
            )
            field_ref[c, pl.ds(2 + 18 * t, 18)] += part.reshape(18, EXT, NZ)

        return some

    def sweep(c, count):
        field = field_ref.at[c]

        def some(t):
            for k in range(count):
                x = 3 + count * t + k
                v1_ref[x] = laplace(field, x)
            for k in range(count):
                x = count * t + k
                value = laplace(v1_ref, x + 2)
                v2_ref[pl.ds(pl.multiple_of(x * EXT, 8), EXT), :] = value
                next_ref[x, c] = value[4:36]

        return some

    def interpolate(c):
        def some(t):
            columns = pl.ds(pl.multiple_of(t * 1024, 1024), 1024)
            mixed = jnp.dot(across_ref[c], plane_ref[:, columns], preferred_element_type=f32)
            total = jnp.sum(mixed * depth_ref[:, columns], axis=0, keepdims=True)
            for k in range(8):
                sum_ref[pl.ds(64 * c + 8 * t + k, 1), :] = total[:, 128 * k : 128 * k + 128]

        return some

    halos = []

    def send_halo(c):
        copies = []
        for k, side in enumerate(SIDES):
            first, last, low, high = side_range(side)
            strips[k][c] = field_ref[c, first:last, low:high, :].reshape(side_rows(side), NZ).astype(bf16)
            copies.append(send(strips[k].at[c], got[k].at[c], around, 8 * c + k, sides[k]))
        halos.append(copies)

    def receive_halo(c):
        for copy in halos[c]:
            copy.wait_recv()
        for side, strip in zip(SIDES, got):
            first, last, low, high = opposite_range(side)
            part = strip[c].astype(f32).reshape(last - first, high - low, NZ)
            field_ref[c, first:last, low:high, :] += part
        for x in (1, 2):
            v1_ref[x] = laplace(field_ref.at[c], x)

    def turn_over(c):
        for part in range(PADDED // 128):
            piece = v2_ref[128 * part : 128 * part + 128, :]
            across_ref[c, :, 128 * part : 128 * part + 128] = piece.T.astype(bf16)

    pass_over(2, [spread(0)])
    send_halo(0)
    pass_over(2, [spread(1)])
    send_halo(1)
    receive_halo(0)
    pass_over(2, [spread(2), sweep(0, 18)])
    send_halo(2)
    turn_over(0)
    receive_halo(1)
    pass_over(6, [interpolate(0), sweep(1, 6)], True)
    turn_over(1)
    receive_halo(2)
    pass_over(6, [interpolate(1), sweep(2, 6)], True)
    turn_over(2)
    own_next = pltpu.make_async_copy(next_ref.at[2:34], next_hbm, bulk.at[2])
    own_next.start()

    def depart(h):
        out_ref[h] = sum_ref[128 * h : 128 * h + 128, :].T.reshape(GY, GX, 128)
        return first_stage("gy", GY, out_ref.at[h], middle_ref.at[h], behind[h], here.at[2 + h])

    def forward():
        for h in range(2):
            for b in range(GY):
                about_ref[h, pl.ds(b, GX, stride=GY), :] = middle_ref[h, b]
        turned = about_ref.reshape(2, GX, GY, 128)
        own = pltpu.make_async_copy(turned.at[:, gx], back_ref.at[:, gx], bulk.at[0])
        copies = []
        for k in range(1, GX):
            peer = lax.rem(gx + k, GX)
            copies.append(send(turned.at[:, peer], back_ref.at[:, gx], behind[2], k, {"gx": peer}))
        own.start()
        return [own], copies

    back = [depart(0)]
    pass_over(6, [interpolate(2)], True)
    back.append(depart(1))
    received(back[0])
    received(back[1])
    back.append(forward())
    received(back[2])
    own_next.wait()
    for stage in [stage1, stage2] + back:
        sent(stage)
    for copies in halos:
        for copy in copies:
            copy.wait_send()


def step(inputs, velocity):
    dma = pltpu.SemaphoreType.DMA
    strips = [pltpu.VMEM((3, side_rows(side), NZ), bf16) for side in SIDES]
    return pl.pallas_call(
        step_kernel,
        out_shape=[
            jax.ShapeDtypeStruct((CELLS, 3, CELLS, NZ), f32),
            jax.ShapeDtypeStruct((2, GX, GY, 128), f32),
        ],
        in_specs=[ANY] * 6,
        out_specs=[ANY, VMEM],
        scratch_shapes=[
            pltpu.VMEM((3, SLOTS), f32),
            pltpu.VMEM((3, SLOTS), f32),
            pltpu.VMEM((3, SLOTS), i32),
            pltpu.VMEM((CAP, 128), i32),
            pltpu.VMEM((1, DEVICES), i32),
            dma((5,)),
            pltpu.VMEM((DEVICES, DEVICES), i32),
            pltpu.VMEM((CAP, 128), f32),
            pltpu.VMEM((6 * CAP, 128), f32),
            pltpu.VMEM((GX * 48, 128), f32),
            pltpu.VMEM((GX, 48, 128), f32),
            pltpu.VMEM((GY * 24, 128), f32),
            pltpu.VMEM((GY, 24, 128), f32),
            pltpu.VMEM((384, 128), f32),
            pltpu.VMEM((12 * CAP, 128), f32),
            pltpu.VMEM((3 * CAP, 128), i32),
            pltpu.VMEM((PADDED, SLOTS), bf16),
            pltpu.VMEM((3, NZ, SLOTS), bf16),
            pltpu.VMEM((NZ, SLOTS), f32),
            pltpu.VMEM((3, EXT, EXT, NZ), f32),
            pltpu.VMEM((EXT, EXT, NZ), f32),
            pltpu.VMEM((PADDED, NZ), f32),
            pltpu.VMEM((3, NZ, PADDED), bf16),
            pltpu.VMEM((256, 128), f32),
            pltpu.VMEM((2, GY, GX, 128), f32),
            pltpu.VMEM((2, GY, GX, 128), f32),
            pltpu.VMEM((2, DEVICES, 128), f32),
            pltpu.VMEM((CELLS, 3, CELLS, NZ), f32),
            pltpu.VMEM((CELLS + 4, 3, CELLS, NZ), f32),
            *strips,
            *strips,
            dma((GX,)), dma((GX,)), dma((GY,)), dma((GY,)),
            dma((GY,)), dma((GY,)), dma((GY,)), dma((GY,)), dma((GX,)), dma((GX,)),
            dma((24,)), dma((24,)), dma((4,)), dma((4,)),
        ],
        compiler_params=params(61, collective_id=0, has_side_effects=True),
        cost_estimate=pl.CostEstimate(flops=4 * PADDED * SLOTS * 3 * NZ, bytes_accessed=10**7, transcendentals=0),
    )(*inputs, velocity)


PIECES = 16


def unpack_kernel(back_hbm, counts_hbm, next_hbm, result_hbm, out_ref, *scratch):
    back_ref, counts_ref, sems, live_ref, flat_ref, next_ref, in_sems, out_sems = scratch
    size = CELLS // PIECES
    pieces = [pl.ds(size * k, size) for k in range(PIECES)]
    arrive = [pltpu.make_async_copy(next_hbm.at[p], next_ref.at[p], in_sems.at[k]) for k, p in enumerate(pieces)]
    leave = [pltpu.make_async_copy(next_ref.at[p], result_hbm.at[p], out_sems.at[k]) for k, p in enumerate(pieces)]
    small = [
        pltpu.make_async_copy(src, dst, sems.at[k])
        for k, (src, dst) in enumerate([(back_hbm, back_ref), (counts_hbm, counts_ref)])
    ]
    for copy in small + arrive:
        copy.start()
    for copy in small:
        copy.wait()
    for k in range(PIECES):
        arrive[k].wait()
        leave[k].start()
    live_ref[...] = counts_column(counts_ref)
    lane = lax.broadcasted_iota(i32, (16, 128), 1)
    for c in range(3):
        base = 64 * (c % 2)
        rows = [jnp.zeros((16, 128), f32)] * 3
        for j in range(8):
            row0, lane0 = divmod(CAP * j, 128)
            part = back_ref[pl.ds(DEVICES * (c // 2) + j, 16, stride=8), :]
            part = jnp.where(lane - base < live_ref[pl.ds(j, 16, stride=8), :], part, 0.0)
            shift = (lane0 - base) % 128
            part = pltpu.roll(part, shift, 1) if shift else part
            rows[row0] = jnp.where((lane >= lane0) & (lane < lane0 + CAP), part, rows[row0])
            if lane0 + CAP > 128:
                rows[row0 + 1] = jnp.where(lane < lane0 + CAP - 128, part, rows[row0 + 1])
        for r in range(3):
            flat_ref[pl.ds(c * CAP + r, 16, stride=3), :] = rows[r]
        for r in range(CAP):
            out_ref[c : c + 1, 128 * r : 128 * r + 128] = flat_ref[c * CAP + r : c * CAP + r + 1, :]
    for copy in leave:
        copy.wait()


def body(velocity, fiber_loads, fractions, corners, neighbours, counts):
    counts = counts.reshape(1, DEVICES)
    dma = pltpu.SemaphoreType.DMA
    inputs = (fiber_loads, fractions, corners, neighbours.reshape(CAP, 128), counts)
    following, back = step(inputs, velocity.transpose(0, 2, 1, 3))
    velocity_next, fiber_velocity = pl.pallas_call(
        unpack_kernel,
        out_shape=[
            jax.ShapeDtypeStruct((CELLS, 3, CELLS, NZ), f32),
            jax.ShapeDtypeStruct((3, SLOTS), f32),
        ],
        in_specs=[HBM] * 3,
        out_specs=[HBM, VMEM],
        scratch_shapes=[
            pltpu.VMEM((2 * DEVICES, 128), f32),
            pltpu.VMEM((1, DEVICES), i32),
            dma((2,)),
            pltpu.VMEM((DEVICES, DEVICES), i32),
            pltpu.VMEM((3 * CAP, 128), f32),
            pltpu.VMEM((CELLS, 3, CELLS, NZ), f32),
            dma((PIECES,)),
            dma((PIECES,)),
        ],
        compiler_params=params(61),
    )(back.reshape(2 * DEVICES, 128), counts, following)
    return (velocity_next.transpose(0, 2, 1, 3), fiber_velocity)


def solution(mesh):
    return jax.shard_map(
        body,
        mesh=mesh,
        in_specs=(
            P("gx", "gy", None, None),
            P(None, ("gx", "gy")),
            P(None, ("gx", "gy")),
            P(None, ("gx", "gy")),
            P(("gx", "gy")),
            P(("gx", "gy")),
        ),
        out_specs=(P("gx", "gy", None, None), P(None, ("gx", "gy"))),
        check_vma=False,
    )
```

```python
import functools

import jax
import jax.numpy as jnp
from jax import lax
from jax.experimental import pallas as pl
from jax.experimental.pallas import tpu as pltpu
from jax.sharding import PartitionSpec as P

viscosity = 0.15
GX, GY = 8, 16
DEVICES = GX * GY
CAP = 48
SLOTS = CAP * DEVICES
CELLS = 32
NZ = 256
EXT = 40
ROWS = 36 * EXT
PADDED = 1536
BLOCKS = CAP // 2
MESH = pl.DeviceIdType.MESH
VMEM = pl.BlockSpec(memory_space=pltpu.VMEM)
ANY = pl.BlockSpec(memory_space=pl.ANY)
HBM = pl.BlockSpec(memory_space=pltpu.MemorySpace.HBM)
f32, bf16, i32 = jnp.float32, jnp.bfloat16, jnp.int32


def params(mib=16, **more):
    return pltpu.CompilerParams(vmem_limit_bytes=mib * 2**20, **more)


def fetch(pairs, sems):
    copies = [pltpu.make_async_copy(src, dst, sems.at[k]) for k, (src, dst) in enumerate(pairs)]
    for copy in copies:
        copy.start()
    for copy in copies:
        copy.wait()


def counts_column(counts_ref):
    return jnp.broadcast_to(counts_ref[...].astype(f32), (DEVICES, DEVICES)).T.astype(i32)


def prepare(loads_ref, frac_ref, corner_ref, partner_ref, counts_ref, live_ref, flat_ref, pos_ref, out_ref):
    live_ref[...] = counts_column(counts_ref)

    def flat_rows(ref, c):
        for r in range(CAP):
            flat_ref[r : r + 1, :] = ref[c : c + 1, 128 * r : 128 * r + 128].astype(f32)
        return flat_ref[...]

    lane = lax.broadcasted_iota(i32, (CAP, 128), 1)
    flat_id = lax.broadcasted_iota(i32, (CAP, 128), 0) * 128 + lane
    bucket = (flat_id * 43691) >> 21
    partner = partner_ref[...]
    high, low = partner >> 7, partner & 127
    whole = (CELLS * GX, CELLS * GY, NZ)
    for c in range(3):
        fraction = flat_rows(frac_ref, c)
        corner = flat_rows(corner_ref, c)
        loads = flat_rows(loads_ref, c)
        position = corner + fraction
        flat_ref[...] = position
        gathered = jnp.zeros((CAP, 128), f32)
        for r in range(CAP):
            row = jnp.broadcast_to(flat_ref[r : r + 1, :], (CAP, 128))
            taken = jnp.take_along_axis(row, low, axis=1, mode="promise_in_bounds")
            gathered = jnp.where(high == r, taken, gathered)
        forcing = loads + (2.0 / whole[c]) * (gathered - position)
        pos_ref[c * CAP : c * CAP + CAP, :] = forcing
        cell = corner.astype(i32)
        if c == 0:
            cell = (cell - (bucket >> 4) * CELLS + 4) & (whole[0] - 1)
        if c == 1:
            cell = (cell - (bucket & 15) * CELLS + 4) & (whole[1] - 1)
        pos_ref[(3 + c) * CAP : (3 + c) * CAP + CAP, :] = cell.astype(f32) + fraction

    lane = lax.broadcasted_iota(i32, (8, 128), 1)
    for j in range(16):
        row0, lane0 = divmod(CAP * j, 128)
        live = (lane & 63) < live_ref[pl.ds(j, 8, stride=16), :]

        def piece(v, target):
            part = pos_ref[pl.ds(v * CAP + row0, 8, stride=6), :]
            if lane0 + CAP > 128:
                later = pos_ref[pl.ds(v * CAP + row0 + 1, 8, stride=6), :]
                part = jnp.where(lane >= lane0, part, later)
            shift = (target - lane0) % 128
            return pltpu.roll(part, shift, 1) if shift else part

        for pair in range(3):
            row = jnp.where(lane < 64, piece(2 * pair, 0), piece(2 * pair + 1, 64))
            if pair == 0:
                row = jnp.where(live, row, 0.0)
            if pair == 1:
                row = jnp.where(live | (lane >= 64), row, 0.0)
            out_ref[pl.ds(16 * pair + j, 8, stride=48), :] = row


def send(src, dst, sems, at, peer):
    copy = pltpu.make_async_remote_copy(
        src_ref=src,
        dst_ref=dst,
        send_sem=sems[0].at[at],
        recv_sem=sems[1].at[at],
        device_id=peer,
        device_id_type=MESH,
    )
    copy.start()
    return copy


def first_stage(axis, count, x_ref, mid_ref, sems, here):
    me = lax.axis_index(axis)
    own = pltpu.make_async_copy(x_ref.at[me], mid_ref.at[me], here)
    copies = []
    for k in range(1, count):
        peer = lax.rem(me + k, count)
        copies.append(send(x_ref.at[peer], mid_ref.at[me], sems, k, {axis: peer}))
    own.start()
    return [own], copies


def received(stage):
    own, copies = stage
    own[0].wait()
    for copy in copies:
        copy.wait_recv()


def sent(stage):
    for copy in stage[1]:
        copy.wait_send()


SIDES = ((-1, 0), (1, 0), (0, -1), (0, 1), (-1, -1), (-1, 1), (1, -1), (1, 1))
LOW, HIGH = (2, 8), (32, 38)


def side_rows(side):
    dx, dy = side
    return 6 * EXT if dy == 0 else 36 * 8 if dx == 0 else 6 * 8


def point_row(ref, base, block):
    return jnp.concatenate([ref[pl.ds(base + 2 * block, 1), :], ref[pl.ds(base + 2 * block + 1, 1), :]], axis=1)


def table(wts_ref, cell_ref, dim, block, length):
    corner = point_row(cell_ref, dim * CAP, block)
    delta = lax.broadcasted_iota(i32, (8, 256), 0) - corner
    weight = jnp.zeros((8, 256), f32)
    for k in range(4):
        weight = jnp.where(delta & 3 == k, point_row(wts_ref, (4 * dim + k) * CAP, block), weight)
    tiles = length // 8
    delta = delta[None] + 8 * lax.broadcasted_iota(i32, (tiles, 8, 256), 0)
    inside = (delta & (NZ - 4 if dim == 2 else -4)) == 0
    return jnp.where(inside, weight[None], 0.0).reshape(length, 256)


def weights(values_ref, wts_ref, cell_ref):
    for dim in range(3):
        position = values_ref[64 * (3 + dim) : 64 * (3 + dim) + CAP, :]
        corner = jnp.floor(position)
        angle = (0.5 * jnp.pi) * (position - corner)
        sine, cosine = jnp.sin(angle), jnp.cos(angle)
        cell_ref[dim * CAP : dim * CAP + CAP, :] = corner.astype(i32)
        for k, term in enumerate((-sine, cosine, sine, -cosine)):
            at = (4 * dim + k) * CAP
            wts_ref[at : at + CAP, :] = 0.25 * (1.0 + term)


def fill_tables(values_ref, wts_ref, cell_ref, plane_ref, push_ref, depth_ref):
    def fill(block, _):
        columns = pl.ds(pl.multiple_of(block * 256, 256), 256)
        along_x = table(wts_ref, cell_ref, 0, block, EXT)
        along_y = table(wts_ref, cell_ref, 1, block, EXT)
        for i in range(18):
            x = 2 + 2 * i
            both = jnp.concatenate([along_y * along_x[x : x + 1], along_y * along_x[x + 1 : x + 2]], axis=0)
            plane_ref[80 * i : 80 * i + 80, columns] = both.astype(bf16)
        depth = table(wts_ref, cell_ref, 2, block, NZ)
        depth_ref[:, columns] = depth
        push_ref[0, :, columns] = (depth * point_row(values_ref, 0, block)).astype(bf16)
        return 0

    lax.fori_loop(0, BLOCKS, fill, 0)


def laplace(ref, x):
    center = ref[x]
    around = ref[x - 1] + ref[x + 1]
    around = around + pltpu.roll(center, 1, 0) + pltpu.roll(center, EXT - 1, 0)
    around = around + pltpu.roll(center, 1, 1) + pltpu.roll(center, NZ - 1, 1)
    return (1.0 - 6.0 * viscosity) * center + viscosity * around


def place_velocity(velocity_ref, field_ref):
    def place(t, _):
        for k in range(4):
            x = 4 * t + k
            for c in range(3):
                field_ref[c, x] = jnp.zeros((EXT, NZ), f32)
        return 0

    lax.fori_loop(0, EXT // 4, place, 0)

    def own(t, _):
        for k in range(4):
            x = 4 * t + k
            for c in range(3):
                field_ref[c, 4 + x, 4:36, :] = velocity_ref[x, c]
        return 0

    lax.fori_loop(0, CELLS // 4, own, 0)


def side_range(side):
    dx, dy = side
    first, last = (2, 38) if dx == 0 else LOW if dx < 0 else HIGH
    low, high = (0, EXT) if dy == 0 else (0, 8) if dy < 0 else (32, 40)
    return first, last, low, high


def opposite_range(side):
    dx, dy = side
    first, last = (2, 38) if dx == 0 else (34, 40) if dx < 0 else (0, 6)
    low, high = (0, EXT) if dy == 0 else (32, 40) if dy < 0 else (0, 8)
    return first, last, low, high


def pass_over(steps, tasks, unroll=False):
    def some(t, _):
        for task in tasks:
            task(t)
        return 0

    lax.fori_loop(0, steps, some, 0, unroll=unroll)


def step_kernel(*refs):
    inputs, velocity_hbm = refs[:5], refs[5]
    next_hbm, back_ref = refs[6:8]
    scratch = refs[8:]
    staged, fetch_sems, (live_ref, flat_ref, pos_ref, payload_ref) = scratch[:5], scratch[5], scratch[6:10]
    mid_ref, turned_ref, recv_ref, values_ref, wts_ref, cell_ref = scratch[10:16]
    plane_ref, push_ref, depth_ref, field_ref, v1_ref, v2_ref, across_ref = scratch[16:23]
    sum_ref, out_ref, middle_ref, about_ref, velocity_ref, next_ref = scratch[23:29]
    strips, got, sems = scratch[29:37], scratch[37:45], scratch[45:]
    ahead, behind, around = (sems[0:2], sems[2:4]), (sems[4:6], sems[6:8], sems[8:10]), sems[10:12]
    here, bulk = sems[12], sems[13]

    gx, gy = lax.axis_index("gx"), lax.axis_index("gy")
    sides = [(lax.rem(gx + dx + GX, GX), lax.rem(gy + dy + GY, GY)) for dx, dy in SIDES]
    peers = [(lax.rem(gx + k, GX), gy) for k in range(1, GX)] + [(gx, lax.rem(gy + k, GY)) for k in range(1, GY)]
    peers = peers + sides[4:]
    barrier = pltpu.get_barrier_semaphore()
    for peer in peers:
        pl.semaphore_signal(barrier, inc=1, device_id=peer, device_id_type=MESH)
    fetch(list(zip(inputs, staged)), fetch_sems)
    own_velocity = pltpu.make_async_copy(velocity_hbm, velocity_ref, bulk.at[3])
    own_velocity.start()
    prepare(*staged, live_ref, flat_ref, pos_ref, payload_ref)
    pl.semaphore_wait(barrier, len(peers))

    stage1 = first_stage("gx", GX, payload_ref.reshape(GX, 48, 128), mid_ref, ahead[0], here.at[0])
    own_velocity.wait()
    place_velocity(velocity_ref, field_ref)
    received(stage1)
    for a in range(GX):
        for pair in range(3):
            turned_ref[pl.ds(8 * pair + a, GY, stride=24), :] = mid_ref[a, 16 * pair : 16 * pair + 16, :]
    stage2 = first_stage("gy", GY, turned_ref.reshape(GY, 24, 128), recv_ref, ahead[1], here.at[1])
    plane_ref[ROWS:, :] = jnp.zeros((PADDED - ROWS, SLOTS), bf16)
    v2_ref[ROWS:, :] = jnp.zeros((PADDED - ROWS, NZ), f32)
    sum_ref[...] = jnp.zeros((256, 128), f32)
    received(stage2)
    for pair in range(3):
        values_ref[128 * pair : 128 * pair + 128, :] = recv_ref[:, 8 * pair : 8 * pair + 8, :].reshape(DEVICES, 128).T
    weights(values_ref, wts_ref, cell_ref)
    fill_tables(values_ref, wts_ref, cell_ref, plane_ref, push_ref, depth_ref)

    def spread(c):
        def some(t):
            part = lax.dot_general(
                plane_ref[pl.ds(pl.multiple_of(720 * t, 720), 720), :],
                push_ref[c],
                (((1,), (1,)), ((), ())),
                preferred_element_type=f32,
            )
            field_ref[c, pl.ds(2 + 18 * t, 18)] += part.reshape(18, EXT, NZ)

        return some

    def push(c):
        def some(t):
            for k in range(BLOCKS // 2):
                block = BLOCKS // 2 * t + k
                columns = pl.ds(pl.multiple_of(block * 256, 256), 256)
                force = point_row(values_ref, 64 * c, block)
                push_ref[c, :, columns] = (depth_ref[:, columns] * force).astype(bf16)

        return some

    def sweep(c, count):
        field = field_ref.at[c]

        def some(t):
            for k in range(count):
                x = 3 + count * t + k
                v1_ref[x] = laplace(field, x)
            for k in range(count):
                x = count * t + k
                value = laplace(v1_ref, x + 2)
                v2_ref[pl.ds(pl.multiple_of(x * EXT, 8), EXT), :] = value
                next_ref[x, c] = value[4:36]

        return some

    def interpolate(c):
        def some(t):
            columns = pl.ds(pl.multiple_of(t * 1024, 1024), 1024)
            mixed = jnp.dot(across_ref[c], plane_ref[:, columns], preferred_element_type=f32)
            total = jnp.sum(mixed * depth_ref[:, columns], axis=0, keepdims=True)
            for k in range(8):
                sum_ref[pl.ds(64 * c + 8 * t + k, 1), :] = total[:, 128 * k : 128 * k + 128]

        return some

    halos = []

    def send_halo(c):
        copies = []
        for k, side in enumerate(SIDES):
            first, last, low, high = side_range(side)
            strips[k][c] = field_ref[c, first:last, low:high, :].reshape(side_rows(side), NZ).astype(bf16)
            copies.append(send(strips[k].at[c], got[k].at[c], around, 8 * c + k, sides[k]))
        halos.append(copies)

    def receive_halo(c):
        for copy in halos[c]:
            copy.wait_recv()
        for side, strip in zip(SIDES, got):
            first, last, low, high = opposite_range(side)
            part = strip[c].astype(f32).reshape(last - first, high - low, NZ)
            field_ref[c, first:last, low:high, :] += part
        for x in (1, 2):
            v1_ref[x] = laplace(field_ref.at[c], x)

    def turn_over(c):
        for part in range(PADDED // 128):
            piece = v2_ref[128 * part : 128 * part + 128, :]
            across_ref[c, :, 128 * part : 128 * part + 128] = piece.T.astype(bf16)

    pass_over(2, [spread(0), push(1)])
    send_halo(0)
    pass_over(2, [spread(1), push(2)])
    send_halo(1)
    receive_halo(0)
    pass_over(2, [spread(2), sweep(0, 18)])
    send_halo(2)
    turn_over(0)
    receive_halo(1)
    pass_over(6, [interpolate(0), sweep(1, 6)], True)
    turn_over(1)
    receive_halo(2)
    pass_over(6, [interpolate(1), sweep(2, 6)], True)
    turn_over(2)
    own_next = pltpu.make_async_copy(next_ref.at[2:34], next_hbm, bulk.at[2])
    own_next.start()

    def depart(h):
        out_ref[h] = sum_ref[128 * h : 128 * h + 128, :].T.reshape(GY, GX, 128)
        return first_stage("gy", GY, out_ref.at[h], middle_ref.at[h], behind[h], here.at[2 + h])

    def forward():
        for h in range(2):
            for b in range(GY):
                about_ref[h, pl.ds(b, GX, stride=GY), :] = middle_ref[h, b]
        turned = about_ref.reshape(2, GX, GY, 128)
        own = pltpu.make_async_copy(turned.at[:, gx], back_ref.at[:, gx], bulk.at[0])
        copies = []
        for k in range(1, GX):
            peer = lax.rem(gx + k, GX)
            copies.append(send(turned.at[:, peer], back_ref.at[:, gx], behind[2], k, {"gx": peer}))
        own.start()
        return [own], copies

    back = [depart(0)]
    pass_over(6, [interpolate(2)], True)
    back.append(depart(1))
    received(back[0])
    received(back[1])
    back.append(forward())
    received(back[2])
    own_next.wait()
    for stage in [stage1, stage2] + back:
        sent(stage)
    for copies in halos:
        for copy in copies:
            copy.wait_send()


def step(inputs, velocity):
    dma = pltpu.SemaphoreType.DMA
    strips = [pltpu.VMEM((3, side_rows(side), NZ), bf16) for side in SIDES]
    return pl.pallas_call(
        step_kernel,
        out_shape=[
            jax.ShapeDtypeStruct((CELLS, 3, CELLS, NZ), f32),
            jax.ShapeDtypeStruct((2, GX, GY, 128), f32),
        ],
        in_specs=[ANY] * 6,
        out_specs=[ANY, VMEM],
        scratch_shapes=[
            pltpu.VMEM((3, SLOTS), f32),
            pltpu.VMEM((3, SLOTS), f32),
            pltpu.VMEM((3, SLOTS), i32),
            pltpu.VMEM((CAP, 128), i32),
            pltpu.VMEM((1, DEVICES), i32),
            dma((5,)),
            pltpu.VMEM((DEVICES, DEVICES), i32),
            pltpu.VMEM((CAP, 128), f32),
            pltpu.VMEM((6 * CAP, 128), f32),
            pltpu.VMEM((GX * 48, 128), f32),
            pltpu.VMEM((GX, 48, 128), f32),
            pltpu.VMEM((GY * 24, 128), f32),
            pltpu.VMEM((GY, 24, 128), f32),
            pltpu.VMEM((384, 128), f32),
            pltpu.VMEM((12 * CAP, 128), f32),
            pltpu.VMEM((3 * CAP, 128), i32),
            pltpu.VMEM((PADDED, SLOTS), bf16),
            pltpu.VMEM((3, NZ, SLOTS), bf16),
            pltpu.VMEM((NZ, SLOTS), f32),
            pltpu.VMEM((3, EXT, EXT, NZ), f32),
            pltpu.VMEM((EXT, EXT, NZ), f32),
            pltpu.VMEM((PADDED, NZ), f32),
            pltpu.VMEM((3, NZ, PADDED), bf16),
            pltpu.VMEM((256, 128), f32),
            pltpu.VMEM((2, GY, GX, 128), f32),
            pltpu.VMEM((2, GY, GX, 128), f32),
            pltpu.VMEM((2, DEVICES, 128), f32),
            pltpu.VMEM((CELLS, 3, CELLS, NZ), f32),
            pltpu.VMEM((CELLS + 4, 3, CELLS, NZ), f32),
            *strips,
            *strips,
            dma((GX,)), dma((GX,)), dma((GY,)), dma((GY,)),
            dma((GY,)), dma((GY,)), dma((GY,)), dma((GY,)), dma((GX,)), dma((GX,)),
            dma((24,)), dma((24,)), dma((4,)), dma((4,)),
        ],
        compiler_params=params(61, collective_id=0, has_side_effects=True),
        cost_estimate=pl.CostEstimate(flops=4 * PADDED * SLOTS * 3 * NZ, bytes_accessed=10**7, transcendentals=0),
    )(*inputs, velocity)


PIECES = 8


def unpack_kernel(back_hbm, counts_hbm, next_hbm, result_hbm, out_hbm, *scratch):
    back_ref, counts_ref, sems, live_ref, flat_ref, next_ref, in_sems, out_sems, out_ref = scratch
    size = CELLS // PIECES
    pieces = [pl.ds(size * k, size) for k in range(PIECES)]
    arrive = [pltpu.make_async_copy(next_hbm.at[p], next_ref.at[p], in_sems.at[k]) for k, p in enumerate(pieces)]
    leave = [pltpu.make_async_copy(next_ref.at[p], result_hbm.at[p], out_sems.at[k]) for k, p in enumerate(pieces)]
    small = [
        pltpu.make_async_copy(src, dst, sems.at[k])
        for k, (src, dst) in enumerate([(back_hbm, back_ref), (counts_hbm, counts_ref)])
    ]
    for copy in small + arrive:
        copy.start()
    for copy in small:
        copy.wait()
    live_ref[...] = counts_column(counts_ref)
    lane = lax.broadcasted_iota(i32, (16, 128), 1)
    for c in range(3):
        base = 64 * (c % 2)
        rows = [jnp.zeros((16, 128), f32)] * 3
        for j in range(8):
            row0, lane0 = divmod(CAP * j, 128)
            part = back_ref[pl.ds(DEVICES * (c // 2) + j, 16, stride=8), :]
            part = jnp.where(lane - base < live_ref[pl.ds(j, 16, stride=8), :], part, 0.0)
            shift = (lane0 - base) % 128
            part = pltpu.roll(part, shift, 1) if shift else part
            rows[row0] = jnp.where((lane >= lane0) & (lane < lane0 + CAP), part, rows[row0])
            if lane0 + CAP > 128:
                rows[row0 + 1] = jnp.where(lane < lane0 + CAP - 128, part, rows[row0 + 1])
        for r in range(3):
            flat_ref[pl.ds(c * CAP + r, 16, stride=3), :] = rows[r]
        for r in range(CAP):
            out_ref[c : c + 1, 128 * r : 128 * r + 128] = flat_ref[c * CAP + r : c * CAP + r + 1, :]
        for k in range(3 * c, min(3 * c + 3, PIECES)):
            arrive[k].wait()
            leave[k].start()
    own = pltpu.make_async_copy(out_ref, out_hbm, sems.at[0])
    own.start()
    for copy in leave + [own]:
        copy.wait()


def body(velocity, fiber_loads, fractions, corners, neighbours, counts):
    counts = counts.reshape(1, DEVICES)
    dma = pltpu.SemaphoreType.DMA
    inputs = (fiber_loads, fractions, corners, neighbours.reshape(CAP, 128), counts)
    following, back = step(inputs, velocity.transpose(0, 2, 1, 3))
    velocity_next, fiber_velocity = pl.pallas_call(
        unpack_kernel,
        out_shape=[
            jax.ShapeDtypeStruct((CELLS, 3, CELLS, NZ), f32),
            jax.ShapeDtypeStruct((3, SLOTS), f32),
        ],
        in_specs=[HBM] * 3,
        out_specs=[HBM, HBM],
        scratch_shapes=[
            pltpu.VMEM((2 * DEVICES, 128), f32),
            pltpu.VMEM((1, DEVICES), i32),
            dma((2,)),
            pltpu.VMEM((DEVICES, DEVICES), i32),
            pltpu.VMEM((3 * CAP, 128), f32),
            pltpu.VMEM((CELLS, 3, CELLS, NZ), f32),
            dma((PIECES,)),
            dma((PIECES,)),
            pltpu.VMEM((3, SLOTS), f32),
        ],
        compiler_params=params(61),
    )(back.reshape(2 * DEVICES, 128), counts, following)
    return (velocity_next.transpose(0, 2, 1, 3), fiber_velocity)


def solution(mesh):
    return jax.shard_map(
        body,
        mesh=mesh,
        in_specs=(
            P("gx", "gy", None, None),
            P(None, ("gx", "gy")),
            P(None, ("gx", "gy")),
            P(None, ("gx", "gy")),
            P(("gx", "gy")),
            P(("gx", "gy")),
        ),
        out_specs=(P("gx", "gy", None, None), P(None, ("gx", "gy"))),
        check_vma=False,
    )
```

```python
import functools

import jax
import jax.numpy as jnp
from jax import lax
from jax.experimental import pallas as pl
from jax.experimental.pallas import tpu as pltpu
from jax.sharding import PartitionSpec as P

viscosity = 0.15
GX, GY = 8, 16
DEVICES = GX * GY
CAP = 48
SLOTS = CAP * DEVICES
CELLS = 32
NZ = 256
EXT = 40
ROWS = 36 * 36
PADDED = 1536
BLOCKS = CAP // 2
MESH = pl.DeviceIdType.MESH
VMEM = pl.BlockSpec(memory_space=pltpu.VMEM)
ANY = pl.BlockSpec(memory_space=pl.ANY)
HBM = pl.BlockSpec(memory_space=pltpu.MemorySpace.HBM)
f32, bf16, i32 = jnp.float32, jnp.bfloat16, jnp.int32


def params(mib=16, **more):
    return pltpu.CompilerParams(vmem_limit_bytes=mib * 2**20, **more)


def fetch(pairs, sems):
    copies = [pltpu.make_async_copy(src, dst, sems.at[k]) for k, (src, dst) in enumerate(pairs)]
    for copy in copies:
        copy.start()
    for copy in copies:
        copy.wait()


def counts_column(counts_ref):
    return jnp.broadcast_to(counts_ref[...].astype(f32), (DEVICES, DEVICES)).T.astype(i32)


def prepare(loads_ref, frac_ref, corner_ref, partner_ref, counts_ref, live_ref, flat_ref, pos_ref, out_ref):
    live_ref[...] = counts_column(counts_ref)

    def flat_rows(ref, c):
        for r in range(CAP):
            flat_ref[r : r + 1, :] = ref[c : c + 1, 128 * r : 128 * r + 128].astype(f32)
        return flat_ref[...]

    lane = lax.broadcasted_iota(i32, (CAP, 128), 1)
    flat_id = lax.broadcasted_iota(i32, (CAP, 128), 0) * 128 + lane
    bucket = (flat_id * 43691) >> 21
    partner = partner_ref[...]
    high, low = partner >> 7, partner & 127
    whole = (CELLS * GX, CELLS * GY, NZ)
    for c in range(3):
        fraction = flat_rows(frac_ref, c)
        corner = flat_rows(corner_ref, c)
        loads = flat_rows(loads_ref, c)
        position = corner + fraction
        flat_ref[...] = position
        gathered = jnp.zeros((CAP, 128), f32)
        for r in range(CAP):
            row = jnp.broadcast_to(flat_ref[r : r + 1, :], (CAP, 128))
            taken = jnp.take_along_axis(row, low, axis=1, mode="promise_in_bounds")
            gathered = jnp.where(high == r, taken, gathered)
        forcing = loads + (2.0 / whole[c]) * (gathered - position)
        pos_ref[c * CAP : c * CAP + CAP, :] = forcing
        cell = corner.astype(i32)
        if c == 0:
            cell = (cell - (bucket >> 4) * CELLS + 4) & (whole[0] - 1)
        if c == 1:
            cell = (cell - (bucket & 15) * CELLS + 4) & (whole[1] - 1)
        pos_ref[(3 + c) * CAP : (3 + c) * CAP + CAP, :] = cell.astype(f32) + fraction

    lane = lax.broadcasted_iota(i32, (8, 128), 1)
    for j in range(16):
        row0, lane0 = divmod(CAP * j, 128)
        live = (lane & 63) < live_ref[pl.ds(j, 8, stride=16), :]

        def piece(v, target):
            part = pos_ref[pl.ds(v * CAP + row0, 8, stride=6), :]
            if lane0 + CAP > 128:
                later = pos_ref[pl.ds(v * CAP + row0 + 1, 8, stride=6), :]
                part = jnp.where(lane >= lane0, part, later)
            shift = (target - lane0) % 128
            return pltpu.roll(part, shift, 1) if shift else part

        for pair in range(3):
            row = jnp.where(lane < 64, piece(2 * pair, 0), piece(2 * pair + 1, 64))
            if pair == 0:
                row = jnp.where(live, row, 0.0)
            if pair == 1:
                row = jnp.where(live | (lane >= 64), row, 0.0)
            out_ref[pl.ds(16 * pair + j, 8, stride=48), :] = row


def send(src, dst, sems, at, peer):
    copy = pltpu.make_async_remote_copy(
        src_ref=src,
        dst_ref=dst,
        send_sem=sems[0].at[at],
        recv_sem=sems[1].at[at],
        device_id=peer,
        device_id_type=MESH,
    )
    copy.start()
    return copy


def first_stage(axis, count, x_ref, mid_ref, sems, here):
    me = lax.axis_index(axis)
    own = pltpu.make_async_copy(x_ref.at[me], mid_ref.at[me], here)
    copies = []
    for k in range(1, count):
        peer = lax.rem(me + k, count)
        copies.append(send(x_ref.at[peer], mid_ref.at[me], sems, k, {axis: peer}))
    own.start()
    return [own], copies


def received(stage):
    own, copies = stage
    own[0].wait()
    for copy in copies:
        copy.wait_recv()


def sent(stage):
    for copy in stage[1]:
        copy.wait_send()


SIDES = ((-1, 0), (1, 0), (0, -1), (0, 1), (-1, -1), (-1, 1), (1, -1), (1, 1))
LOW, HIGH = (2, 8), (32, 38)


def side_rows(side):
    dx, dy = side
    return 6 * EXT if dy == 0 else 36 * 8 if dx == 0 else 6 * 8


def point_row(ref, base, block):
    return jnp.concatenate([ref[pl.ds(base + 2 * block, 1), :], ref[pl.ds(base + 2 * block + 1, 1), :]], axis=1)


def table(wts_ref, cell_ref, dim, block, length, first=0):
    corner = point_row(cell_ref, dim * CAP, block)
    delta = lax.broadcasted_iota(i32, (8, 256), 0) + first - corner
    weight = jnp.zeros((8, 256), f32)
    for k in range(4):
        weight = jnp.where(delta & 3 == k, point_row(wts_ref, (4 * dim + k) * CAP, block), weight)
    tiles = length // 8
    delta = delta[None] + 8 * lax.broadcasted_iota(i32, (tiles, 8, 256), 0)
    inside = (delta & (NZ - 4 if dim == 2 else -4)) == 0
    return jnp.where(inside, weight[None], 0.0).reshape(length, 256)


def weights(values_ref, wts_ref, cell_ref):
    for dim in range(3):
        position = values_ref[64 * (3 + dim) : 64 * (3 + dim) + CAP, :]
        corner = jnp.floor(position)
        angle = (0.5 * jnp.pi) * (position - corner)
        sine, cosine = jnp.sin(angle), jnp.cos(angle)
        cell_ref[dim * CAP : dim * CAP + CAP, :] = corner.astype(i32)
        for k, term in enumerate((-sine, cosine, sine, -cosine)):
            at = (4 * dim + k) * CAP
            wts_ref[at : at + CAP, :] = 0.25 * (1.0 + term)


def fill_tables(values_ref, wts_ref, cell_ref, plane_ref, push_ref, depth_ref):
    def fill(block, _):
        columns = pl.ds(pl.multiple_of(block * 256, 256), 256)
        along_x = table(wts_ref, cell_ref, 0, block, EXT)
        even_y = table(wts_ref, cell_ref, 1, block, EXT, 2)
        odd_y = table(wts_ref, cell_ref, 1, block, EXT, -2)
        for i in range(9):
            parts = []
            for x in (2 + 4 * i, 4 + 4 * i):
                even, odd = along_x[x : x + 1], along_x[x + 1 : x + 2]
                parts += [even_y[:32] * even, even_y[32:] * even + odd_y[:8] * odd, odd_y[8:] * odd]
            plane_ref[144 * i : 144 * i + 144, columns] = jnp.concatenate(parts, axis=0).astype(bf16)
        depth = table(wts_ref, cell_ref, 2, block, NZ)
        depth_ref[:, columns] = depth
        push_ref[0, :, columns] = (depth * point_row(values_ref, 0, block)).astype(bf16)
        return 0

    lax.fori_loop(0, BLOCKS, fill, 0)


def laplace(ref, x):
    center = ref[x]
    around = ref[x - 1] + ref[x + 1]
    around = around + pltpu.roll(center, 1, 0) + pltpu.roll(center, EXT - 1, 0)
    around = around + pltpu.roll(center, 1, 1) + pltpu.roll(center, NZ - 1, 1)
    return (1.0 - 6.0 * viscosity) * center + viscosity * around


def place_velocity(velocity_ref, field_ref):
    def place(t, _):
        for k in range(4):
            x = 4 * t + k
            for c in range(3):
                field_ref[c, x] = jnp.zeros((EXT, NZ), f32)
        return 0

    lax.fori_loop(0, EXT // 4, place, 0)

    def own(t, _):
        for k in range(4):
            x = 4 * t + k
            for c in range(3):
                field_ref[c, 4 + x, 4:36, :] = velocity_ref[x, c]
        return 0

    lax.fori_loop(0, CELLS // 4, own, 0)


def side_range(side):
    dx, dy = side
    first, last = (2, 38) if dx == 0 else LOW if dx < 0 else HIGH
    low, high = (0, EXT) if dy == 0 else (0, 8) if dy < 0 else (32, 40)
    return first, last, low, high


def opposite_range(side):
    dx, dy = side
    first, last = (2, 38) if dx == 0 else (34, 40) if dx < 0 else (0, 6)
    low, high = (0, EXT) if dy == 0 else (32, 40) if dy < 0 else (0, 8)
    return first, last, low, high


def pass_over(steps, tasks, unroll=False):
    def some(t, _):
        for task in tasks:
            task(t)
        return 0

    lax.fori_loop(0, steps, some, 0, unroll=unroll)


def step_kernel(*refs):
    inputs, velocity_hbm = refs[:5], refs[5]
    next_hbm, back_ref = refs[6:8]
    scratch = refs[8:]
    staged, fetch_sems, (live_ref, flat_ref, pos_ref, payload_ref) = scratch[:5], scratch[5], scratch[6:10]
    mid_ref, turned_ref, recv_ref, values_ref, wts_ref, cell_ref = scratch[10:16]
    plane_ref, push_ref, depth_ref, field_ref, v1_ref, v2_ref, across_ref = scratch[16:23]
    sum_ref, out_ref, middle_ref, about_ref, velocity_ref, next_ref = scratch[23:29]
    strips, got, sems = scratch[29:37], scratch[37:45], scratch[45:]
    ahead, behind, around = (sems[0:2], sems[2:4]), (sems[4:6], sems[6:8], sems[8:10]), sems[10:12]
    here, bulk = sems[12], sems[13]

    gx, gy = lax.axis_index("gx"), lax.axis_index("gy")
    sides = [(lax.rem(gx + dx + GX, GX), lax.rem(gy + dy + GY, GY)) for dx, dy in SIDES]
    peers = [(lax.rem(gx + k, GX), gy) for k in range(1, GX)] + [(gx, lax.rem(gy + k, GY)) for k in range(1, GY)]
    peers = peers + sides[4:]
    barrier = pltpu.get_barrier_semaphore()
    for peer in peers:
        pl.semaphore_signal(barrier, inc=1, device_id=peer, device_id_type=MESH)
    fetch(list(zip(inputs, staged)), fetch_sems)
    own_velocity = pltpu.make_async_copy(velocity_hbm, velocity_ref, bulk.at[3])
    own_velocity.start()
    prepare(*staged, live_ref, flat_ref, pos_ref, payload_ref)
    pl.semaphore_wait(barrier, len(peers))

    stage1 = first_stage("gx", GX, payload_ref.reshape(GX, 48, 128), mid_ref, ahead[0], here.at[0])
    own_velocity.wait()
    place_velocity(velocity_ref, field_ref)
    received(stage1)
    for a in range(GX):
        for pair in range(3):
            turned_ref[pl.ds(8 * pair + a, GY, stride=24), :] = mid_ref[a, 16 * pair : 16 * pair + 16, :]
    stage2 = first_stage("gy", GY, turned_ref.reshape(GY, 24, 128), recv_ref, ahead[1], here.at[1])
    plane_ref[ROWS:, :] = jnp.zeros((PADDED - ROWS, SLOTS), bf16)
    v2_ref[18:] = jnp.zeros((4, 72, NZ), f32)
    sum_ref[...] = jnp.zeros((256, 128), f32)
    received(stage2)
    for pair in range(3):
        values_ref[128 * pair : 128 * pair + 128, :] = recv_ref[:, 8 * pair : 8 * pair + 8, :].reshape(DEVICES, 128).T
    weights(values_ref, wts_ref, cell_ref)
    fill_tables(values_ref, wts_ref, cell_ref, plane_ref, push_ref, depth_ref)

    def spread(c):
        def some(t):
            part = lax.dot_general(
                plane_ref[pl.ds(pl.multiple_of(432 * t, 432), 432), :],
                push_ref[c],
                (((1,), (1,)), ((), ())),
                preferred_element_type=f32,
            )
            for k in range(12):
                field_ref[c, 2 + 12 * t + k, 2:38, :] += part[36 * k : 36 * k + 36]

        return some

    def push(c):
        def some(t):
            for k in range(BLOCKS // 3):
                block = BLOCKS // 3 * t + k
                columns = pl.ds(pl.multiple_of(block * 256, 256), 256)
                force = point_row(values_ref, 64 * c, block)
                push_ref[c, :, columns] = (depth_ref[:, columns] * force).astype(bf16)

        return some

    def sweep(c, count):
        field = field_ref.at[c]

        def some(t):
            for k in range(count):
                x = 3 + count * t + k
                v1_ref[x] = laplace(field, x)
            for k in range(count):
                x = count * t + k
                value = laplace(v1_ref, x + 2)
                v2_ref[count // 2 * t + k // 2, 36 * (k % 2) : 36 * (k % 2) + 36] = value[2:38]
                next_ref[x, c] = value[4:36]

        return some

    def interpolate(c):
        def some(t):
            columns = pl.ds(pl.multiple_of(t * 1024, 1024), 1024)
            mixed = jnp.dot(across_ref[c], plane_ref[:, columns], preferred_element_type=f32)
            total = jnp.sum(mixed * depth_ref[:, columns], axis=0, keepdims=True)
            for k in range(8):
                sum_ref[pl.ds(64 * c + 8 * t + k, 1), :] = total[:, 128 * k : 128 * k + 128]

        return some

    halos = []

    def send_halo(c):
        copies = []
        for k, side in enumerate(SIDES):
            first, last, low, high = side_range(side)
            strips[k][c] = field_ref[c, first:last, low:high, :].reshape(side_rows(side), NZ).astype(bf16)
            copies.append(send(strips[k].at[c], got[k].at[c], around, 8 * c + k, sides[k]))
        halos.append(copies)

    def receive_halo(c):
        for copy in halos[c]:
            copy.wait_recv()
        for side, strip in zip(SIDES, got):
            first, last, low, high = opposite_range(side)
            part = strip[c].astype(f32).reshape(last - first, high - low, NZ)
            field_ref[c, first:last, low:high, :] += part
        for x in (1, 2):
            v1_ref[x] = laplace(field_ref.at[c], x)

    def turn_over(c):
        for part in range(PADDED // 128):
            piece = v2_ref.reshape(22 * 72, NZ)[128 * part : 128 * part + 128, :]
            across_ref[c, :, 128 * part : 128 * part + 128] = piece.T.astype(bf16)

    pass_over(3, [spread(0), push(1)])
    send_halo(0)
    pass_over(3, [spread(1), push(2)])
    send_halo(1)
    receive_halo(0)
    pass_over(3, [spread(2), sweep(0, 12)], True)
    send_halo(2)
    turn_over(0)
    receive_halo(1)
    pass_over(6, [interpolate(0), sweep(1, 6)], True)
    turn_over(1)
    receive_halo(2)
    pass_over(6, [interpolate(1), sweep(2, 6)], True)
    turn_over(2)
    own_next = pltpu.make_async_copy(next_ref.at[2:34], next_hbm, bulk.at[2])
    own_next.start()

    def depart(h):
        out_ref[h] = sum_ref[128 * h : 128 * h + 128, :].T.reshape(GY, GX, 128)
        return first_stage("gy", GY, out_ref.at[h], middle_ref.at[h], behind[h], here.at[2 + h])

    def forward():
        for h in range(2):
            for b in range(GY):
                about_ref[h, pl.ds(b, GX, stride=GY), :] = middle_ref[h, b]
        turned = about_ref.reshape(2, GX, GY, 128)
        own = pltpu.make_async_copy(turned.at[:, gx], back_ref.at[:, gx], bulk.at[0])
        copies = []
        for k in range(1, GX):
            peer = lax.rem(gx + k, GX)
            copies.append(send(turned.at[:, peer], back_ref.at[:, gx], behind[2], k, {"gx": peer}))
        own.start()
        return [own], copies

    back = [depart(0)]
    pass_over(6, [interpolate(2)], True)
    back.append(depart(1))
    received(back[0])
    received(back[1])
    back.append(forward())
    received(back[2])
    own_next.wait()
    for stage in [stage1, stage2] + back:
        sent(stage)
    for copies in halos:
        for copy in copies:
            copy.wait_send()


def step(inputs, velocity):
    dma = pltpu.SemaphoreType.DMA
    strips = [pltpu.VMEM((3, side_rows(side), NZ), bf16) for side in SIDES]
    return pl.pallas_call(
        step_kernel,
        out_shape=[
            jax.ShapeDtypeStruct((CELLS, 3, CELLS, NZ), f32),
            jax.ShapeDtypeStruct((2, GX, GY, 128), f32),
        ],
        in_specs=[ANY] * 6,
        out_specs=[ANY, VMEM],
        scratch_shapes=[
            pltpu.VMEM((3, SLOTS), f32),
            pltpu.VMEM((3, SLOTS), f32),
            pltpu.VMEM((3, SLOTS), i32),
            pltpu.VMEM((CAP, 128), i32),
            pltpu.VMEM((1, DEVICES), i32),
            dma((5,)),
            pltpu.VMEM((DEVICES, DEVICES), i32),
            pltpu.VMEM((CAP, 128), f32),
            pltpu.VMEM((6 * CAP, 128), f32),
            pltpu.VMEM((GX * 48, 128), f32),
            pltpu.VMEM((GX, 48, 128), f32),
            pltpu.VMEM((GY * 24, 128), f32),
            pltpu.VMEM((GY, 24, 128), f32),
            pltpu.VMEM((384, 128), f32),
            pltpu.VMEM((12 * CAP, 128), f32),
            pltpu.VMEM((3 * CAP, 128), i32),
            pltpu.VMEM((PADDED, SLOTS), bf16),
            pltpu.VMEM((3, NZ, SLOTS), bf16),
            pltpu.VMEM((NZ, SLOTS), f32),
            pltpu.VMEM((3, EXT, EXT, NZ), f32),
            pltpu.VMEM((EXT, EXT, NZ), f32),
            pltpu.VMEM((22, 72, NZ), f32),
            pltpu.VMEM((3, NZ, PADDED), bf16),
            pltpu.VMEM((256, 128), f32),
            pltpu.VMEM((2, GY, GX, 128), f32),
            pltpu.VMEM((2, GY, GX, 128), f32),
            pltpu.VMEM((2, DEVICES, 128), f32),
            pltpu.VMEM((CELLS, 3, CELLS, NZ), f32),
            pltpu.VMEM((CELLS + 4, 3, CELLS, NZ), f32),
            *strips,
            *strips,
            dma((GX,)), dma((GX,)), dma((GY,)), dma((GY,)),
            dma((GY,)), dma((GY,)), dma((GY,)), dma((GY,)), dma((GX,)), dma((GX,)),
            dma((24,)), dma((24,)), dma((4,)), dma((4,)),
        ],
        compiler_params=params(61, collective_id=0, has_side_effects=True),
        cost_estimate=pl.CostEstimate(flops=4 * PADDED * SLOTS * 3 * NZ, bytes_accessed=10**7, transcendentals=0),
    )(*inputs, velocity)


PIECES = 8


def unpack_kernel(back_hbm, counts_hbm, next_hbm, result_hbm, out_hbm, *scratch):
    back_ref, counts_ref, sems, live_ref, flat_ref, next_ref, in_sems, out_sems, out_ref = scratch
    size = CELLS // PIECES
    pieces = [pl.ds(size * k, size) for k in range(PIECES)]
    arrive = [pltpu.make_async_copy(next_hbm.at[p], next_ref.at[p], in_sems.at[k]) for k, p in enumerate(pieces)]
    leave = [pltpu.make_async_copy(next_ref.at[p], result_hbm.at[p], out_sems.at[k]) for k, p in enumerate(pieces)]
    small = [
        pltpu.make_async_copy(src, dst, sems.at[k])
        for k, (src, dst) in enumerate([(back_hbm, back_ref), (counts_hbm, counts_ref)])
    ]
    for copy in small + arrive:
        copy.start()
    for copy in small:
        copy.wait()
    live_ref[...] = counts_column(counts_ref)
    lane = lax.broadcasted_iota(i32, (16, 128), 1)
    for c in range(3):
        base = 64 * (c % 2)
        rows = [jnp.zeros((16, 128), f32)] * 3
        for j in range(8):
            row0, lane0 = divmod(CAP * j, 128)
            part = back_ref[pl.ds(DEVICES * (c // 2) + j, 16, stride=8), :]
            part = jnp.where(lane - base < live_ref[pl.ds(j, 16, stride=8), :], part, 0.0)
            shift = (lane0 - base) % 128
            part = pltpu.roll(part, shift, 1) if shift else part
            rows[row0] = jnp.where((lane >= lane0) & (lane < lane0 + CAP), part, rows[row0])
            if lane0 + CAP > 128:
                rows[row0 + 1] = jnp.where(lane < lane0 + CAP - 128, part, rows[row0 + 1])
        for r in range(3):
            flat_ref[pl.ds(c * CAP + r, 16, stride=3), :] = rows[r]
        for r in range(CAP):
            out_ref[c : c + 1, 128 * r : 128 * r + 128] = flat_ref[c * CAP + r : c * CAP + r + 1, :]
        for k in range(3 * c, min(3 * c + 3, PIECES)):
            arrive[k].wait()
            leave[k].start()
    own = pltpu.make_async_copy(out_ref, out_hbm, sems.at[0])
    own.start()
    for copy in leave + [own]:
        copy.wait()


def body(velocity, fiber_loads, fractions, corners, neighbours, counts):
    counts = counts.reshape(1, DEVICES)
    dma = pltpu.SemaphoreType.DMA
    inputs = (fiber_loads, fractions, corners, neighbours.reshape(CAP, 128), counts)
    following, back = step(inputs, velocity.transpose(0, 2, 1, 3))
    velocity_next, fiber_velocity = pl.pallas_call(
        unpack_kernel,
        out_shape=[
            jax.ShapeDtypeStruct((CELLS, 3, CELLS, NZ), f32),
            jax.ShapeDtypeStruct((3, SLOTS), f32),
        ],
        in_specs=[HBM] * 3,
        out_specs=[HBM, HBM],
        scratch_shapes=[
            pltpu.VMEM((2 * DEVICES, 128), f32),
            pltpu.VMEM((1, DEVICES), i32),
            dma((2,)),
            pltpu.VMEM((DEVICES, DEVICES), i32),
            pltpu.VMEM((3 * CAP, 128), f32),
            pltpu.VMEM((CELLS, 3, CELLS, NZ), f32),
            dma((PIECES,)),
            dma((PIECES,)),
            pltpu.VMEM((3, SLOTS), f32),
        ],
        compiler_params=params(61),
    )(back.reshape(2 * DEVICES, 128), counts, following)
    return (velocity_next.transpose(0, 2, 1, 3), fiber_velocity)


def solution(mesh):
    return jax.shard_map(
        body,
        mesh=mesh,
        in_specs=(
            P("gx", "gy", None, None),
            P(None, ("gx", "gy")),
            P(None, ("gx", "gy")),
            P(None, ("gx", "gy")),
            P(("gx", "gy")),
            P(("gx", "gy")),
        ),
        out_specs=(P("gx", "gy", None, None), P(None, ("gx", "gy"))),
        check_vma=False,
    )
```

```python
import functools

import jax
import jax.numpy as jnp
from jax import lax
from jax.experimental import pallas as pl
from jax.experimental.pallas import tpu as pltpu
from jax.sharding import PartitionSpec as P

viscosity = 0.15
GX, GY = 8, 16
DEVICES = GX * GY
CAP = 48
SLOTS = CAP * DEVICES
CELLS = 32
NZ = 256
EXT = 40
ROWS = 36 * 36
PADDED = 1536
BLOCKS = CAP // 2
MESH = pl.DeviceIdType.MESH
VMEM = pl.BlockSpec(memory_space=pltpu.VMEM)
ANY = pl.BlockSpec(memory_space=pl.ANY)
HBM = pl.BlockSpec(memory_space=pltpu.MemorySpace.HBM)
f32, bf16, i32 = jnp.float32, jnp.bfloat16, jnp.int32


def params(mib=16, **more):
    return pltpu.CompilerParams(vmem_limit_bytes=mib * 2**20, **more)


def fetch(pairs, sems):
    copies = [pltpu.make_async_copy(src, dst, sems.at[k]) for k, (src, dst) in enumerate(pairs)]
    for copy in copies:
        copy.start()
    for copy in copies:
        copy.wait()


def counts_column(counts_ref):
    return jnp.broadcast_to(counts_ref[...].astype(f32), (DEVICES, DEVICES)).T.astype(i32)


def prepare(loads_ref, frac_ref, corner_ref, partner_ref, counts_ref, live_ref, flat_ref, pos_ref, out_ref):
    live_ref[...] = counts_column(counts_ref)

    def flat_rows(ref, c):
        for r in range(CAP):
            flat_ref[r : r + 1, :] = ref[c : c + 1, 128 * r : 128 * r + 128].astype(f32)
        return flat_ref[...]

    lane = lax.broadcasted_iota(i32, (CAP, 128), 1)
    flat_id = lax.broadcasted_iota(i32, (CAP, 128), 0) * 128 + lane
    bucket = (flat_id * 43691) >> 21
    partner = partner_ref[...]
    high, low = partner >> 7, partner & 127
    whole = (CELLS * GX, CELLS * GY, NZ)
    for c in range(3):
        fraction = flat_rows(frac_ref, c)
        corner = flat_rows(corner_ref, c)
        loads = flat_rows(loads_ref, c)
        position = corner + fraction
        flat_ref[...] = position
        gathered = jnp.zeros((CAP, 128), f32)
        for r in range(CAP):
            row = jnp.broadcast_to(flat_ref[r : r + 1, :], (CAP, 128))
            taken = jnp.take_along_axis(row, low, axis=1, mode="promise_in_bounds")
            gathered = jnp.where(high == r, taken, gathered)
        forcing = loads + (2.0 / whole[c]) * (gathered - position)
        pos_ref[c * CAP : c * CAP + CAP, :] = forcing
        cell = corner.astype(i32)
        if c == 0:
            cell = (cell - (bucket >> 4) * CELLS + 4) & (whole[0] - 1)
        if c == 1:
            cell = (cell - (bucket & 15) * CELLS + 4) & (whole[1] - 1)
        pos_ref[(3 + c) * CAP : (3 + c) * CAP + CAP, :] = cell.astype(f32) + fraction

    lane = lax.broadcasted_iota(i32, (8, 128), 1)
    for j in range(16):
        row0, lane0 = divmod(CAP * j, 128)
        live = (lane & 63) < live_ref[pl.ds(j, 8, stride=16), :]

        def piece(v, target):
            part = pos_ref[pl.ds(v * CAP + row0, 8, stride=6), :]
            if lane0 + CAP > 128:
                later = pos_ref[pl.ds(v * CAP + row0 + 1, 8, stride=6), :]
                part = jnp.where(lane >= lane0, part, later)
            shift = (target - lane0) % 128
            return pltpu.roll(part, shift, 1) if shift else part

        for pair in range(3):
            row = jnp.where(lane < 64, piece(2 * pair, 0), piece(2 * pair + 1, 64))
            if pair == 0:
                row = jnp.where(live, row, 0.0)
            if pair == 1:
                row = jnp.where(live | (lane >= 64), row, 0.0)
            out_ref[pl.ds(16 * pair + j, 8, stride=48), :] = row


def send(src, dst, sems, at, peer):
    copy = pltpu.make_async_remote_copy(
        src_ref=src,
        dst_ref=dst,
        send_sem=sems[0].at[at],
        recv_sem=sems[1].at[at],
        device_id=peer,
        device_id_type=MESH,
    )
    copy.start()
    return copy


def first_stage(axis, count, x_ref, mid_ref, sems, here):
    me = lax.axis_index(axis)
    own = pltpu.make_async_copy(x_ref.at[me], mid_ref.at[me], here)
    copies = []
    for k in range(1, count):
        peer = lax.rem(me + k, count)
        copies.append(send(x_ref.at[peer], mid_ref.at[me], sems, k, {axis: peer}))
    own.start()
    return [own], copies


def received(stage):
    own, copies = stage
    own[0].wait()
    for copy in copies:
        copy.wait_recv()


def sent(stage):
    for copy in stage[1]:
        copy.wait_send()


SIDES = ((-1, 0), (1, 0), (0, -1), (0, 1), (-1, -1), (-1, 1), (1, -1), (1, 1))
LOW, HIGH = (2, 8), (32, 38)


def side_rows(side):
    dx, dy = side
    return 6 * EXT if dy == 0 else 224 if dx == 0 else 6 * 8


def point_row(ref, base, block):
    return jnp.concatenate([ref[pl.ds(base + 2 * block, 1), :], ref[pl.ds(base + 2 * block + 1, 1), :]], axis=1)


def table(wts_ref, cell_ref, dim, block, length, first=0):
    corner = point_row(cell_ref, dim * CAP, block)
    delta = lax.broadcasted_iota(i32, (8, 256), 0) + first - corner
    weight = jnp.zeros((8, 256), f32)
    for k in range(4):
        weight = jnp.where(delta & 3 == k, point_row(wts_ref, (4 * dim + k) * CAP, block), weight)
    tiles = length // 8
    delta = delta[None] + 8 * lax.broadcasted_iota(i32, (tiles, 8, 256), 0)
    inside = (delta & (NZ - 4 if dim == 2 else -4)) == 0
    return jnp.where(inside, weight[None], 0.0).reshape(length, 256)


def weights(values_ref, wts_ref, cell_ref):
    for dim in range(3):
        position = values_ref[64 * (3 + dim) : 64 * (3 + dim) + CAP, :]
        corner = jnp.floor(position)
        angle = (0.5 * jnp.pi) * (position - corner)
        sine, cosine = jnp.sin(angle), jnp.cos(angle)
        cell_ref[dim * CAP : dim * CAP + CAP, :] = corner.astype(i32)
        for k, term in enumerate((-sine, cosine, sine, -cosine)):
            at = (4 * dim + k) * CAP
            wts_ref[at : at + CAP, :] = 0.25 * (1.0 + term)


def fill_tables(values_ref, wts_ref, cell_ref, plane_ref, push_ref, depth_ref):
    def fill(block, _):
        columns = pl.ds(pl.multiple_of(block * 256, 256), 256)
        along_x = table(wts_ref, cell_ref, 0, block, EXT)
        even_y = table(wts_ref, cell_ref, 1, block, EXT, 2)
        odd_y = table(wts_ref, cell_ref, 1, block, EXT, -2)
        for i in range(9):
            parts = []
            for x in (2 + 4 * i, 4 + 4 * i):
                even, odd = along_x[x : x + 1], along_x[x + 1 : x + 2]
                parts += [even_y[:32] * even, even_y[32:] * even + odd_y[:8] * odd, odd_y[8:] * odd]
            plane_ref[144 * i : 144 * i + 144, columns] = jnp.concatenate(parts, axis=0).astype(bf16)
        depth = table(wts_ref, cell_ref, 2, block, NZ)
        depth_ref[:, columns] = depth
        push_ref[0, :, columns] = (depth * point_row(values_ref, 0, block)).astype(bf16)
        return 0

    lax.fori_loop(0, BLOCKS, fill, 0)


def laplace(ref, x):
    center = ref[x]
    around = ref[x - 1] + ref[x + 1]
    around = around + pltpu.roll(center, 1, 0) + pltpu.roll(center, EXT - 1, 0)
    around = around + pltpu.roll(center, 1, 1) + pltpu.roll(center, NZ - 1, 1)
    return (1.0 - 6.0 * viscosity) * center + viscosity * around


def place_velocity(velocity_ref, field_ref):
    def place(t, _):
        for k in range(4):
            x = 4 * t + k
            for c in range(3):
                field_ref[c, x] = jnp.zeros((EXT, NZ), f32)
        return 0

    lax.fori_loop(0, EXT // 4, place, 0)

    def own(t, _):
        for k in range(4):
            x = 4 * t + k
            for c in range(3):
                field_ref[c, 4 + x, 4:36, :] = velocity_ref[x, c]
        return 0

    lax.fori_loop(0, CELLS // 4, own, 0)


def side_range(side):
    dx, dy = side
    first, last = (2, 38) if dx == 0 else LOW if dx < 0 else HIGH
    low, high = (0, EXT) if dy == 0 else (0, 8) if dy < 0 else (32, 40)
    return first, last, low, high


def opposite_range(side):
    dx, dy = side
    first, last = (2, 38) if dx == 0 else (34, 40) if dx < 0 else (0, 6)
    low, high = (0, EXT) if dy == 0 else (32, 40) if dy < 0 else (0, 8)
    return first, last, low, high


def pass_over(steps, tasks, unroll=False):
    def some(t, _):
        for task in tasks:
            task(t)
        return 0

    lax.fori_loop(0, steps, some, 0, unroll=unroll)


def step_kernel(*refs):
    inputs, velocity_hbm = refs[:5], refs[5]
    next_hbm, back_ref = refs[6:8]
    scratch = refs[8:]
    staged, fetch_sems, (live_ref, flat_ref, pos_ref, payload_ref) = scratch[:5], scratch[5], scratch[6:10]
    mid_ref, turned_ref, recv_ref, values_ref, wts_ref, cell_ref = scratch[10:16]
    plane_ref, push_ref, depth_ref, field_ref, v1_ref, v2_ref, across_ref = scratch[16:23]
    sum_ref, out_ref, middle_ref, about_ref, velocity_ref, next_ref = scratch[23:29]
    strips, got, sems = scratch[29:37], scratch[37:45], scratch[45:]
    ahead, behind, around = (sems[0:2], sems[2:4]), (sems[4:6], sems[6:8], sems[8:10]), sems[10:12]
    here, bulk = sems[12], sems[13]

    gx, gy = lax.axis_index("gx"), lax.axis_index("gy")
    sides = [(lax.rem(gx + dx + GX, GX), lax.rem(gy + dy + GY, GY)) for dx, dy in SIDES]
    peers = [(lax.rem(gx + k, GX), gy) for k in range(1, GX)] + [(gx, lax.rem(gy + k, GY)) for k in range(1, GY)]
    peers = peers + sides[4:]
    barrier = pltpu.get_barrier_semaphore()
    for peer in peers:
        pl.semaphore_signal(barrier, inc=1, device_id=peer, device_id_type=MESH)
    fetch(list(zip(inputs, staged)), fetch_sems)
    own_velocity = pltpu.make_async_copy(velocity_hbm, velocity_ref, bulk.at[3])
    own_velocity.start()
    prepare(*staged, live_ref, flat_ref, pos_ref, payload_ref)
    pl.semaphore_wait(barrier, len(peers))

    stage1 = first_stage("gx", GX, payload_ref.reshape(GX, 48, 128), mid_ref, ahead[0], here.at[0])
    own_velocity.wait()
    place_velocity(velocity_ref, field_ref)
    received(stage1)
    for a in range(GX):
        for pair in range(3):
            turned_ref[pl.ds(8 * pair + a, GY, stride=24), :] = mid_ref[a, 16 * pair : 16 * pair + 16, :]
    stage2 = first_stage("gy", GY, turned_ref.reshape(GY, 24, 128), recv_ref, ahead[1], here.at[1])
    plane_ref[ROWS:, :] = jnp.zeros((PADDED - ROWS, SLOTS), bf16)
    v2_ref[18:] = jnp.zeros((4, 72, NZ), f32)
    sum_ref[...] = jnp.zeros((256, 128), f32)
    received(stage2)
    for pair in range(3):
        values_ref[128 * pair : 128 * pair + 128, :] = recv_ref[:, 8 * pair : 8 * pair + 8, :].reshape(DEVICES, 128).T
    weights(values_ref, wts_ref, cell_ref)
    fill_tables(values_ref, wts_ref, cell_ref, plane_ref, push_ref, depth_ref)

    def spread(c):
        def some(t):
            part = lax.dot_general(
                plane_ref[pl.ds(pl.multiple_of(432 * t, 432), 432), :],
                push_ref[c],
                (((1,), (1,)), ((), ())),
                preferred_element_type=f32,
            )
            for k in range(12):
                field_ref[c, 2 + 12 * t + k, 2:38, :] += part[36 * k : 36 * k + 36]

        return some

    def push(c):
        def some(t):
            for k in range(BLOCKS // 3):
                block = BLOCKS // 3 * t + k
                columns = pl.ds(pl.multiple_of(block * 256, 256), 256)
                force = point_row(values_ref, 64 * c, block)
                push_ref[c, :, columns] = (depth_ref[:, columns] * force).astype(bf16)

        return some

    def sweep(c, count):
        field = field_ref.at[c]

        def some(t):
            for k in range(count):
                x = 3 + count * t + k
                v1_ref[x] = laplace(field, x)
            for k in range(count):
                x = count * t + k
                value = laplace(v1_ref, x + 2)
                v2_ref[count // 2 * t + k // 2, 36 * (k % 2) : 36 * (k % 2) + 36] = value[2:38]
                next_ref[x, c] = value[4:36]

        return some

    def interpolate(c):
        def some(t):
            columns = pl.ds(pl.multiple_of(t * 1024, 1024), 1024)
            mixed = jnp.dot(across_ref[c], plane_ref[:, columns], preferred_element_type=f32)
            total = jnp.sum(mixed * depth_ref[:, columns], axis=0, keepdims=True)
            for k in range(8):
                sum_ref[pl.ds(64 * c + 8 * t + k, 1), :] = total[:, 128 * k : 128 * k + 128]

        return some

    halos = []

    def send_halo(c):
        copies = []
        for k, side in enumerate(SIDES):
            first, last, low, high = side_range(side)
            if side[0] == 0:
                low = 2 if side[1] < 0 else 32
                parts = [field_ref[c, x, low : low + 6, :] for x in range(2, 38)] + [jnp.zeros((8, NZ), f32)]
                strips[k][c] = jnp.concatenate(parts, axis=0).astype(bf16)
            else:
                strips[k][c] = field_ref[c, first:last, low:high, :].reshape(side_rows(side), NZ).astype(bf16)
            copies.append(send(strips[k].at[c], got[k].at[c], around, 8 * c + k, sides[k]))
        halos.append(copies)

    def receive_halo(c):
        for copy in halos[c]:
            copy.wait_recv()
        for side, strip in zip(SIDES, got):
            first, last, low, high = opposite_range(side)
            part = strip[c].astype(f32)
            if side[0] == 0:
                low = 34 if side[1] < 0 else 0
                for x in range(36):
                    field_ref[c, 2 + x, low : low + 6, :] += part[6 * x : 6 * x + 6]
            else:
                field_ref[c, first:last, low:high, :] += part.reshape(last - first, high - low, NZ)
        for x in (1, 2):
            v1_ref[x] = laplace(field_ref.at[c], x)

    def turn_over(c):
        for part in range(PADDED // 128):
            piece = v2_ref.reshape(22 * 72, NZ)[128 * part : 128 * part + 128, :]
            across_ref[c, :, 128 * part : 128 * part + 128] = piece.T.astype(bf16)

    pass_over(3, [spread(0), push(1)])
    send_halo(0)
    pass_over(3, [spread(1), push(2)])
    send_halo(1)
    receive_halo(0)
    pass_over(3, [spread(2), sweep(0, 12)], True)
    send_halo(2)
    turn_over(0)
    receive_halo(1)
    pass_over(6, [interpolate(0), sweep(1, 6)], True)
    turn_over(1)
    receive_halo(2)
    pass_over(6, [interpolate(1), sweep(2, 6)], True)
    turn_over(2)
    own_next = pltpu.make_async_copy(next_ref.at[2:34], next_hbm, bulk.at[2])
    own_next.start()

    def depart(h):
        out_ref[h] = sum_ref[128 * h : 128 * h + 128, :].T.reshape(GY, GX, 128)
        return first_stage("gy", GY, out_ref.at[h], middle_ref.at[h], behind[h], here.at[2 + h])

    def forward():
        for h in range(2):
            for b in range(GY):
                about_ref[h, pl.ds(b, GX, stride=GY), :] = middle_ref[h, b]
        turned = about_ref.reshape(2, GX, GY, 128)
        own = pltpu.make_async_copy(turned.at[:, gx], back_ref.at[:, gx], bulk.at[0])
        copies = []
        for k in range(1, GX):
            peer = lax.rem(gx + k, GX)
            copies.append(send(turned.at[:, peer], back_ref.at[:, gx], behind[2], k, {"gx": peer}))
        own.start()
        return [own], copies

    back = [depart(0)]
    pass_over(6, [interpolate(2)], True)
    back.append(depart(1))
    received(back[0])
    received(back[1])
    back.append(forward())
    received(back[2])
    own_next.wait()
    for stage in [stage1, stage2] + back:
        sent(stage)
    for copies in halos:
        for copy in copies:
            copy.wait_send()


def step(inputs, velocity):
    dma = pltpu.SemaphoreType.DMA
    strips = [pltpu.VMEM((3, side_rows(side), NZ), bf16) for side in SIDES]
    return pl.pallas_call(
        step_kernel,
        out_shape=[
            jax.ShapeDtypeStruct((CELLS, 3, CELLS, NZ), f32),
            jax.ShapeDtypeStruct((2, GX, GY, 128), f32),
        ],
        in_specs=[ANY] * 6,
        out_specs=[ANY, VMEM],
        scratch_shapes=[
            pltpu.VMEM((3, SLOTS), f32),
            pltpu.VMEM((3, SLOTS), f32),
            pltpu.VMEM((3, SLOTS), i32),
            pltpu.VMEM((CAP, 128), i32),
            pltpu.VMEM((1, DEVICES), i32),
            dma((5,)),
            pltpu.VMEM((DEVICES, DEVICES), i32),
            pltpu.VMEM((CAP, 128), f32),
            pltpu.VMEM((6 * CAP, 128), f32),
            pltpu.VMEM((GX * 48, 128), f32),
            pltpu.VMEM((GX, 48, 128), f32),
            pltpu.VMEM((GY * 24, 128), f32),
            pltpu.VMEM((GY, 24, 128), f32),
            pltpu.VMEM((384, 128), f32),
            pltpu.VMEM((12 * CAP, 128), f32),
            pltpu.VMEM((3 * CAP, 128), i32),
            pltpu.VMEM((PADDED, SLOTS), bf16),
            pltpu.VMEM((3, NZ, SLOTS), bf16),
            pltpu.VMEM((NZ, SLOTS), f32),
            pltpu.VMEM((3, EXT, EXT, NZ), f32),
            pltpu.VMEM((EXT, EXT, NZ), f32),
            pltpu.VMEM((22, 72, NZ), f32),
            pltpu.VMEM((3, NZ, PADDED), bf16),
            pltpu.VMEM((256, 128), f32),
            pltpu.VMEM((2, GY, GX, 128), f32),
            pltpu.VMEM((2, GY, GX, 128), f32),
            pltpu.VMEM((2, DEVICES, 128), f32),
            pltpu.VMEM((CELLS, 3, CELLS, NZ), f32),
            pltpu.VMEM((CELLS + 4, 3, CELLS, NZ), f32),
            *strips,
            *strips,
            dma((GX,)), dma((GX,)), dma((GY,)), dma((GY,)),
            dma((GY,)), dma((GY,)), dma((GY,)), dma((GY,)), dma((GX,)), dma((GX,)),
            dma((24,)), dma((24,)), dma((4,)), dma((4,)),
        ],
        compiler_params=params(61, collective_id=0, has_side_effects=True),
        cost_estimate=pl.CostEstimate(flops=4 * PADDED * SLOTS * 3 * NZ, bytes_accessed=10**7, transcendentals=0),
    )(*inputs, velocity)


PIECES = 8


def unpack_kernel(back_hbm, counts_hbm, next_hbm, result_hbm, out_hbm, *scratch):
    back_ref, counts_ref, sems, live_ref, flat_ref, next_ref, in_sems, out_sems, out_ref = scratch
    size = CELLS // PIECES
    pieces = [pl.ds(size * k, size) for k in range(PIECES)]
    arrive = [pltpu.make_async_copy(next_hbm.at[p], next_ref.at[p], in_sems.at[k]) for k, p in enumerate(pieces)]
    leave = [pltpu.make_async_copy(next_ref.at[p], result_hbm.at[p], out_sems.at[k]) for k, p in enumerate(pieces)]
    small = [
        pltpu.make_async_copy(src, dst, sems.at[k])
        for k, (src, dst) in enumerate([(back_hbm, back_ref), (counts_hbm, counts_ref)])
    ]
    for copy in small + arrive:
        copy.start()
    for copy in small:
        copy.wait()
    live_ref[...] = counts_column(counts_ref)
    lane = lax.broadcasted_iota(i32, (16, 128), 1)
    for c in range(3):
        base = 64 * (c % 2)
        rows = [jnp.zeros((16, 128), f32)] * 3
        for j in range(8):
            row0, lane0 = divmod(CAP * j, 128)
            part = back_ref[pl.ds(DEVICES * (c // 2) + j, 16, stride=8), :]
            part = jnp.where(lane - base < live_ref[pl.ds(j, 16, stride=8), :], part, 0.0)
            shift = (lane0 - base) % 128
            part = pltpu.roll(part, shift, 1) if shift else part
            rows[row0] = jnp.where((lane >= lane0) & (lane < lane0 + CAP), part, rows[row0])
            if lane0 + CAP > 128:
                rows[row0 + 1] = jnp.where(lane < lane0 + CAP - 128, part, rows[row0 + 1])
        for r in range(3):
            flat_ref[pl.ds(c * CAP + r, 16, stride=3), :] = rows[r]
        for r in range(CAP):
            out_ref[c : c + 1, 128 * r : 128 * r + 128] = flat_ref[c * CAP + r : c * CAP + r + 1, :]
        for k in range(3 * c, min(3 * c + 3, PIECES)):
            arrive[k].wait()
            leave[k].start()
    own = pltpu.make_async_copy(out_ref, out_hbm, sems.at[0])
    own.start()
    for copy in leave + [own]:
        copy.wait()


def body(velocity, fiber_loads, fractions, corners, neighbours, counts):
    counts = counts.reshape(1, DEVICES)
    dma = pltpu.SemaphoreType.DMA
    inputs = (fiber_loads, fractions, corners, neighbours.reshape(CAP, 128), counts)
    following, back = step(inputs, velocity.transpose(0, 2, 1, 3))
    velocity_next, fiber_velocity = pl.pallas_call(
        unpack_kernel,
        out_shape=[
            jax.ShapeDtypeStruct((CELLS, 3, CELLS, NZ), f32),
            jax.ShapeDtypeStruct((3, SLOTS), f32),
        ],
        in_specs=[HBM] * 3,
        out_specs=[HBM, HBM],
        scratch_shapes=[
            pltpu.VMEM((2 * DEVICES, 128), f32),
            pltpu.VMEM((1, DEVICES), i32),
            dma((2,)),
            pltpu.VMEM((DEVICES, DEVICES), i32),
            pltpu.VMEM((3 * CAP, 128), f32),
            pltpu.VMEM((CELLS, 3, CELLS, NZ), f32),
            dma((PIECES,)),
            dma((PIECES,)),
            pltpu.VMEM((3, SLOTS), f32),
        ],
        compiler_params=params(61),
    )(back.reshape(2 * DEVICES, 128), counts, following)
    return (velocity_next.transpose(0, 2, 1, 3), fiber_velocity)


def solution(mesh):
    return jax.shard_map(
        body,
        mesh=mesh,
        in_specs=(
            P("gx", "gy", None, None),
            P(None, ("gx", "gy")),
            P(None, ("gx", "gy")),
            P(None, ("gx", "gy")),
            P(("gx", "gy")),
            P(("gx", "gy")),
        ),
        out_specs=(P("gx", "gy", None, None), P(None, ("gx", "gy"))),
        check_vma=False,
    )
```
